32 devices in a mesh: ma: 4 (over y, x), mb: 8 (over z, core).
Axes of the slice: x: 2, y: 2, z: 4, core: 2. Of those that a mesh axis runs over, the one named last changes fastest.
Arguments:
- tier_four: float32 [256, 2, 128, 128], P(('ma', 'mb')), may hold values from -6 to 6
- tier_six: float32 [256, 2, 128, 128], P(('ma', 'mb')), may hold values from -6 to 6
- tier_seven: float32 [256, 2, 128, 128], P(('ma', 'mb')), may hold values from -6 to 6
- coupling: float32 [128, 128], replicated
- eigenbasis: float32 [128, 128], replicated
- energies: float32 [128], replicated, may hold values from -6 to 6
- decay_rates: float32 [12], replicated, may hold values from 0.5 to 4
- bath_coefficients: float32 [2, 12], replicated, may hold values from -1 to 1
- occupation_five: int32 [256, 12], P(('ma', 'mb')), may hold values from 0 to 5, as said below
- local_five: int32 [256, 2, 9], P(('ma', 'mb')), may hold values from 0 to 7
- peers_five: int32 [256, 4], P(('ma', 'mb')), may hold values from 0 to 7, all different within a row; in each aligned block of 8 rows (0 to 7, 8 to 15, ...) at most 6 rows name the same one
- places_five: int32 [256, 4], P(('ma', 'mb')), may hold values from 0 to 7
- occupation_six: int32 [256, 12], P(('ma', 'mb')), may hold values from 0 to 6, as said below
- local_six: int32 [256, 2, 9], P(('ma', 'mb')), may hold values from 0 to 7
- peers_six: int32 [256, 4], P(('ma', 'mb')), may hold values from 0 to 7, all different within a row; in each aligned block of 8 rows (0 to 7, 8 to 15, ...) at most 6 rows name the same one
- places_six: int32 [256, 4], P(('ma', 'mb')), may hold values from 0 to 7
Outputs:
- updated_five: float32 [256, 2, 128, 128], P(('ma', 'mb'))
- updated_six: float32 [256, 2, 128, 128], P(('ma', 'mb'))
The draws below stay inside these ranges and needn't reach their ends.
Inputs may be any that keep to these rules, and one draw needn't show every extreme that they name: `occupation_five`: each row sums to 5; the first row of every block of 8 rows has all 5 in one mode. `occupation_six`: each row sums to 6; the first row of every block of 8 rows has all 6 in one mode. `local_five`: positions within the matrix's own block of 8 rows; a lowered entry is read only where its mode's occupation is positive. `local_six`: positions within the matrix's own block of 8 rows; a lowered entry is read only where its mode's occupation is positive. `peers_five`: the four entries of a row differ; among the rows of one block of 8 rows no value appears more than 6 times, and some value appears exactly 6 times. `peers_six`: the four entries of a row differ; among the rows of one block of 8 rows no value appears more than 6 times, and some value appears exactly 6 times.
All inputs are finite; a program needn't handle non-finite values.
Results may differ from the reference program's by a relative error of at most 0.0003.
Values sent between devices are 32-bit elements; how exact they have to be, the bound alone decides.
No kernel may reach another device: no remote copies, remote signals or barrier semaphores. Data moves between devices by JAX's collectives and lax.ppermute only.
A program may use at most 128 MiB of HBM per device.

```python
import math
import jax
import jax.numpy as jnp
import numpy as np
from jax import lax

NB = 128
K = 12
M_DEV = 8
CAP = 6
M_ALL = 256
LOCAL_MODES = 9
N_MA = 4
N_MB = 8


def occupations(key, tier_count):
    picks = jax.random.randint(key, (M_ALL, tier_count), 0, K)
    leading = jnp.arange(M_ALL, dtype=jnp.int32)[:, None] % M_DEV == 0
    picks = jnp.where(leading, picks[:, :1], picks)
    return jnp.sum((picks[:, :, None] == jnp.arange(K, dtype=jnp.int32)[None, None, :]).astype(jnp.int32), axis=1)


def draw_occupation_five(key, part):
    return occupations(jax.random.fold_in(key, 41), 5)


def draw_occupation_six(key, part):
    return occupations(jax.random.fold_in(key, 53), 6)


def draw_coupling(key, part):
    raw_entries = jax.random.normal(jax.random.fold_in(key, 7), (NB, NB), jnp.float32)
    return (raw_entries + jnp.transpose(raw_entries)) / jnp.sqrt(2.0 * NB)


def draw_eigenbasis(key, part):
    mirrors = jax.random.normal(jax.random.fold_in(key, 11), (NB, NB), jnp.float32)

    def reflect(turn_index, frames):
        mirror = mirrors[turn_index]
        image_vec = jnp.dot(frames, mirror, precision=lax.Precision.HIGHEST)
        return frames - 2.0 * jnp.outer(image_vec, mirror) / jnp.sum(mirror * mirror)
    return lax.fori_loop(0, NB, reflect, jnp.eye(NB, dtype=jnp.float32))


def set_ends(array, stream_key, least, largest):
    longest = array.shape.index(max(array.shape))
    spots = []
    for shift in (0, 1):
        where = [jax.random.randint(jax.random.fold_in(stream_key, axis), (), 0, length) for axis, length in enumerate(array.shape)]
        where[longest] = (where[longest] + shift) % array.shape[longest]
        spots.append(tuple(where))
    return array.at[spots[0]].set(least).at[spots[1]].set(largest)


def block_scale(key, dims, cuts, least, top_value):
    gain, own = 1.0, jax.random.fold_in(key, 6)
    for dim, shards_of in cuts:
        draws = jnp.exp(jax.random.uniform(jax.random.fold_in(own, dim), (shards_of,), jnp.float32, least / len(cuts), top_value / len(cuts)))
        gain = gain * jnp.repeat(draws, dims[dim] // shards_of).reshape([-1 if axis == dim else 1 for axis in range(len(dims))])
    return gain


def shared_out(key, own, number, rows, count, top, reach, lean):
    order = jax.random.permutation(key, count)
    packed, common = load_shares(count, rows * top, reach, lean, True), load_shares(count, rows * top, reach, lean, False)
    places = jnp.arange(count)

    def named(tallies, turn):
        used = int((tallies > 0).sum())
        fixed = max(1, used // 4)
        shifted = fixed + (places - fixed + turn * (used - fixed)) % max(1, count - fixed)
        return jnp.zeros((count,), jnp.int32).at[order[jnp.where(places < fixed, places, shifted)]].set(jnp.asarray(tallies, jnp.int32))

    tallies = jnp.where(number % 4 == 0, named(packed, number // 4), named(common, number - number // 4 - 1))
    mixed = jax.random.permutation(jax.random.fold_in(own, 3), count)
    giver, taker = mixed[0:count // 2 * 2:2], mixed[1:count // 2 * 2:2]
    slack = jnp.minimum(tallies[giver] - 1, reach - tallies[taker]) // 2
    slack = jnp.where((giver == order[0]) | (taker == order[0]) | (tallies[taker] == 0), 0, jnp.maximum(slack, 0))
    shifted = jax.random.randint(jax.random.fold_in(own, 4), (count // 2,), 0, 1 << 20) % (slack + 1)
    tallies = tallies.at[giver].add(-shifted).at[taker].add(shifted)
    items = jnp.searchsorted(jnp.cumsum(tallies), jnp.arange(rows * top), side="right").astype(jnp.int32)
    listing = items.reshape(top, rows).T
    listing = listing[jax.random.permutation(jax.random.fold_in(own, 1), rows)]
    turn = jax.random.randint(jax.random.fold_in(own, 2), (rows, 1), 0, top)
    return jnp.take_along_axis(listing, (jnp.arange(top)[None, :] + turn) % top, axis=1)


def load_shares(number_of, total, reach, lean, full):
    weights = [(1 << 20) // math.isqrt(grade ** lean) + 1 for grade in range(1, number_of + 1)]
    largest = reach if full else min(reach, max(-(-total // number_of), total * weights[0] // sum(weights)))
    least = 1 if total - largest >= number_of - 1 else 0
    holding, surplus = [largest] + [least] * (number_of - 1), total - largest - least * (number_of - 1)
    while surplus > 0:
        candidates = [i for i in range(1, number_of) if holding[i] < largest] or [i for i in range(1, number_of) if holding[i] < reach]
        mass, remaining = sum([weights[i] for i in candidates]), surplus
        for i in candidates:
            extra = min(reach - holding[i], max(1, remaining * weights[i] // mass), surplus)
            holding[i] = holding[i] + extra
            surplus = surplus - extra
    return np.array(holding)


def scatter_about(rng, shape, scale, limit, cuts=(), kind=jnp.bfloat16):
    array = jax.random.normal(rng, shape, jnp.float32) * scale
    if len(cuts) > 0:
        array = block_scale(rng, shape, cuts, -0.22, 0.18) * array
    return jnp.clip(array, min=-limit, max=limit).astype(kind)


def setup_inputs(seed: int = 0) -> dict:
    arg_keys = jax.random.split(jax.random.key(seed), 17)
    tier_four = scatter_about(arg_keys[0], (M_ALL, 2, NB, NB), 1.0, 6.0, ((0, 32),), jnp.float32)
    tier_six = scatter_about(arg_keys[1], (M_ALL, 2, NB, NB), 1.0, 6.0, ((0, 32),), jnp.float32)
    tier_seven = scatter_about(arg_keys[2], (M_ALL, 2, NB, NB), 1.0, 6.0, ((0, 32),), jnp.float32)
    coupling = draw_coupling(jax.random.fold_in(arg_keys[16], 71), 0)
    eigenbasis = draw_eigenbasis(jax.random.fold_in(arg_keys[16], 71), 0)
    energies = jnp.clip(jax.random.uniform(arg_keys[5], (NB,), jnp.float32, -6.0, 6.0), -6.0, 6.0)
    decay_rates = jnp.clip(jnp.exp(jax.random.uniform(arg_keys[6], (K,), jnp.float32, math.log(0.5), math.log(4.0))), 0.5, 4.0)
    bath_coefficients = jnp.clip(jax.random.uniform(arg_keys[7], (2, K), jnp.float32, -1.0, 1.0), -1.0, 1.0)
    occupation_five = draw_occupation_five(jax.random.fold_in(arg_keys[16], 71), 0)
    local_five = set_ends(jax.random.randint(arg_keys[9], (M_ALL, 2, LOCAL_MODES), 0, M_DEV), jax.random.fold_in(arg_keys[9], 1), 0, M_DEV - 1).astype(jnp.int32)
    peers_five_keys = jax.random.split(jax.random.fold_in(arg_keys[10], 1), M_ALL // M_DEV)
    peers_five_turns = jax.random.permutation(jax.random.fold_in(arg_keys[10], 3), M_ALL // M_DEV)
    peers_five = jax.vmap(lambda own, number: shared_out(jax.random.fold_in(arg_keys[10], 2), own, number, M_DEV, N_MB, 4, CAP, 2))(peers_five_keys, peers_five_turns).reshape((M_ALL, 4))
    places_five = set_ends(jax.random.randint(arg_keys[11], (M_ALL, 4), 0, M_DEV), jax.random.fold_in(arg_keys[11], 1), 0, M_DEV - 1).astype(jnp.int32)
    occupation_six = draw_occupation_six(jax.random.fold_in(arg_keys[16], 71), 0)
    local_six = set_ends(jax.random.randint(arg_keys[13], (M_ALL, 2, LOCAL_MODES), 0, M_DEV), jax.random.fold_in(arg_keys[13], 1), 0, M_DEV - 1).astype(jnp.int32)
    peers_six_keys = jax.random.split(jax.random.fold_in(arg_keys[14], 1), M_ALL // M_DEV)
    peers_six_turns = jax.random.permutation(jax.random.fold_in(arg_keys[14], 3), M_ALL // M_DEV)
    peers_six = jax.vmap(lambda own, number: shared_out(jax.random.fold_in(arg_keys[14], 2), own, number, M_DEV, N_MB, 4, CAP, 2))(peers_six_keys, peers_six_turns).reshape((M_ALL, 4))
    places_six = set_ends(jax.random.randint(arg_keys[15], (M_ALL, 4), 0, M_DEV), jax.random.fold_in(arg_keys[15], 1), 0, M_DEV - 1).astype(jnp.int32)
    return dict(tier_four=tier_four, tier_six=tier_six, tier_seven=tier_seven, coupling=coupling, eigenbasis=eigenbasis, energies=energies, decay_rates=decay_rates, bath_coefficients=bath_coefficients, occupation_five=occupation_five, local_five=local_five, peers_five=peers_five, places_five=places_five, occupation_six=occupation_six, local_six=local_six, peers_six=peers_six, places_six=places_six)


HIGHEST = lax.Precision.HIGHEST


def left_product(matrix, batch):
    return jnp.einsum('ij,mjk->mik', matrix, batch, precision=HIGHEST)


def right_product(batch, matrix):
    return jnp.einsum('mij,jk->mik', batch, matrix, precision=HIGHEST)


def mix_terms(up_real, up_imag, sum_rr, sum_ri, sum_ir, sum_ii):
    return (up_real + sum_rr - sum_ii, up_imag + sum_ri + sum_ir,
            up_real + sum_rr + sum_ii, up_imag + sum_ri - sum_ir)


def settle(pair_real, pair_imag, other_real, other_imag, occupation, coupling, eigenbasis, energies, decay_rates):
    comm_real = left_product(coupling, pair_real) - right_product(other_real, coupling)
    comm_imag = left_product(coupling, pair_imag) - right_product(other_imag, coupling)
    turned = jnp.transpose(eigenbasis)
    eigen_real = right_product(left_product(turned, -comm_imag), eigenbasis)
    eigen_imag = right_product(left_product(turned, comm_real), eigenbasis)
    damping = jnp.dot(occupation.astype(jnp.float32), decay_rates, precision=HIGHEST)[:, None, None]
    splitting = (energies[:, None] - energies[None, :])[None]
    denominator = damping * damping + splitting * splitting
    factor_real = -damping / denominator
    factor_imag = splitting / denominator
    solved_real = eigen_real * factor_real - eigen_imag * factor_imag
    solved_imag = eigen_real * factor_imag + eigen_imag * factor_real
    back_real = right_product(left_product(eigenbasis, solved_real), turned)
    back_imag = right_product(left_product(eigenbasis, solved_imag), turned)
    return jnp.stack([back_real, back_imag], axis=1)


def sweep_tier(lower_tier, upper_tier, local_table, peer_table, place_table, occupation,
               bath_coefficients, coupling, eigenbasis, energies, decay_rates):
    def one_device(device):
        row_major = device // N_MB
        row_minor = device % N_MB
        first_row = device * M_DEV
        within = jnp.arange(M_DEV, dtype=jnp.int32)
        raised_first = (((row_major + 1) % N_MA) * N_MB + row_minor) * M_DEV + within
        lowered_first = (((row_major + N_MA - 1) % N_MA) * N_MB + row_minor) * M_DEV + within
        nearby = lax.dynamic_slice_in_dim(local_table, first_row, M_DEV, 0)
        peer_ids = lax.dynamic_slice_in_dim(peer_table, first_row, M_DEV, 0)
        places = lax.dynamic_slice_in_dim(place_table, first_row, M_DEV, 0)
        counted = lax.dynamic_slice_in_dim(occupation, first_row, M_DEV, 0)
        remote = ((row_major * N_MB + peer_ids) * M_DEV + places).astype(jnp.int32)
        raised = jnp.concatenate([raised_first[:, None], remote[:, :2], first_row + nearby[:, 0, :]], axis=1)
        lowered = jnp.concatenate([lowered_first[:, None], remote[:, 2:], first_row + nearby[:, 1, :]], axis=1)
        up_sum = jnp.sum(upper_tier[raised], axis=1)
        lower_mats = lower_tier[lowered]
        weight_real = counted.astype(jnp.float32) * bath_coefficients[0][None, :]
        weight_imag = counted.astype(jnp.float32) * bath_coefficients[1][None, :]

        def weighted(weights, part_index):
            return jnp.einsum('mk,mkij->mij', weights, lower_mats[:, :, part_index], precision=HIGHEST)

        pair_real, pair_imag, other_real, other_imag = mix_terms(
            up_sum[:, 0], up_sum[:, 1], weighted(weight_real, 0), weighted(weight_real, 1),
            weighted(weight_imag, 0), weighted(weight_imag, 1))
        return settle(pair_real, pair_imag, other_real, other_imag, counted,
                      coupling, eigenbasis, energies, decay_rates)

    blocks = lax.map(one_device, jnp.arange(N_MA * N_MB, dtype=jnp.int32))
    return blocks.reshape(lower_tier.shape)


def reference(tier_four, tier_six, tier_seven, coupling, eigenbasis, energies, decay_rates, bath_coefficients,
              occupation_five, local_five, peers_five, places_five,
              occupation_six, local_six, peers_six, places_six):
    updated_five = sweep_tier(tier_four, tier_six, local_five, peers_five, places_five, occupation_five,
                              bath_coefficients, coupling, eigenbasis, energies, decay_rates)
    updated_six = sweep_tier(updated_five, tier_seven, local_six, peers_six, places_six, occupation_six,
                             bath_coefficients, coupling, eigenbasis, energies, decay_rates)
    return updated_five, updated_six
```

```python
import functools

import jax
import jax.numpy as jnp
from jax import lax
from jax.experimental import pallas as pl
from jax.experimental.pallas import tpu as pltpu
from jax.sharding import PartitionSpec as P

SMEM = pltpu.SMEM
VMEM = pltpu.VMEM
HALVES = 2


def split(x):
    high = x.astype(jnp.bfloat16)
    return high, (x - high.astype(jnp.float32)).astype(jnp.bfloat16)


def as_left(w):
    high, low = split(w)
    return jnp.concatenate([high, high, low], axis=1)


def as_right(w):
    high, low = split(w)
    return jnp.concatenate([high, high, low], axis=0)


def left_dot(w_left, x):
    high, low = split(x)
    return jnp.dot(
        w_left, jnp.concatenate([high, low, high], axis=0), preferred_element_type=jnp.float32
    )


def right_dot(x, w_right):
    high, low = split(x)
    return jnp.dot(
        jnp.concatenate([high, low, high], axis=1), w_right, preferred_element_type=jnp.float32
    )


def sandwich(w_left, real, imag, w_right):
    n = real.shape[0]
    right = right_dot(jnp.concatenate([real, imag], axis=0), w_right)
    both = left_dot(w_left, jnp.concatenate([right[:n], right[n:]], axis=1))
    return both[:, :n], both[:, n:]


def drive_of(mixed, turned, c_left, c_right):
    n = mixed.shape[-1]
    ahead = left_dot(
        c_left, jnp.concatenate([mixed[1] + turned[0], mixed[0] - turned[1]], axis=1)
    )
    behind = right_dot(
        jnp.concatenate([mixed[1] - turned[0], mixed[0] + turned[1]], axis=0), c_right
    )
    return behind[:n] - ahead[:, :n], ahead[:, n:] - behind[n:]


def add_requests(
    row, column, target, rows, place, table, bath, upper, lower, mixed, turned
):
    chip = place[0]
    core = place[1]
    for j in range(4):
        peer = table[target, column + row * 4 + j]
        spot = table[target, column + rows * 4 + row * 4 + j]
        here = peer >> 1 == chip
        for sibling in range(2):
            own = (peer & 1 == core) if sibling == 0 else (peer & 1 != core)

            @pl.when(jnp.logical_and(here, own))
            def _(j=j, sibling=sibling, spot=spot):
                if j < 2:
                    mixed[...] += upper[sibling][spot]
                else:
                    mode = j - 1
                    count = table[target, column + rows * 8 + row * 2 + j - 2].astype(jnp.float32)
                    source = lower[sibling][spot]
                    mixed[...] += (count * bath[0, mode]) * source
                    turned[...] += (count * bath[1, mode]) * source


def partial_kernel(
    slot, column, place, table, bath, upper_own, upper_sib, lower_own, lower_sib, c_ref, *rest
):
    outs, (mixed, turned) = rest[:-2], rest[-2:]
    rows = upper_own.shape[0]
    target = place[2 + slot]
    c_left = as_left(c_ref[...])
    c_right = as_right(c_ref[...])
    per = rows // len(outs)
    for half, out in enumerate(outs):

        @pl.loop(0, per)
        def _(m, half=half, out=out):
            mixed[...] = jnp.zeros_like(mixed)
            turned[...] = jnp.zeros_like(turned)
            add_requests(
                half * per + m,
                column,
                target,
                rows,
                place,
                table,
                bath,
                (upper_own, upper_sib),
                (lower_own, lower_sib),
                mixed,
                turned,
            )
            real, imag = drive_of(mixed[...], turned[...], c_left, c_right)
            out[m, 0] = real
            out[m, 1] = imag


def own_kernel(
    slot,
    column,
    place,
    table,
    bath,
    nearby,
    occupation,
    upper_own,
    upper_sib,
    lower_own,
    lower_sib,
    raised,
    lowered,
    c_ref,
    out,
    mixed,
    turned,
):
    rows = upper_own.shape[0]
    modes = bath.shape[1]
    target = place[2 + slot]
    c_left = as_left(c_ref[...])
    c_right = as_right(c_ref[...])

    @pl.loop(0, rows)
    def _(m):
        count = occupation[m, 0].astype(jnp.float32)
        below = lowered[m]
        mixed[...] = raised[m] + (count * bath[0, 0]) * below
        turned[...] = (count * bath[1, 0]) * below
        add_requests(
            m,
            column,
            target,
            rows,
            place,
            table,
            bath,
            (upper_own, upper_sib),
            (lower_own, lower_sib),
            mixed,
            turned,
        )
        for k in range(3, modes):
            mixed[...] += upper_own[nearby[m, k - 3]]
            held = occupation[m, k]

            @pl.when(held > 0)
            def _(k=k, held=held):
                source = lower_own[nearby[m, modes - 3 + k - 3]]
                mixed[...] += (held.astype(jnp.float32) * bath[0, k]) * source
                turned[...] += (held.astype(jnp.float32) * bath[1, k]) * source

        real, imag = drive_of(mixed[...], turned[...], c_left, c_right)
        out[m, 0] = real
        out[m, 1] = imag


def solved(real, imag, damping, splitting):
    inverse = 1.0 / (damping * damping + splitting * splitting)
    factor_real = -damping * inverse
    factor_imag = splitting * inverse
    return real * factor_real - imag * factor_imag, real * factor_imag + imag * factor_real


def solve_kernel(
    arrivals, turn_in, turn_out, occupation, decay, e_row, e_column, e_ref, et_ref, own, *rest
):
    parts, outs = rest[:arrivals], rest[arrivals:]
    rows = own.shape[0]
    splitting = e_column[...] - e_row[...]
    if turn_in:
        in_left = as_left(et_ref[...])
        in_right = as_right(e_ref[...])
    if turn_out:
        out_left = as_left(e_ref[...])
        out_right = as_right(et_ref[...])
    per = parts[0].shape[0]
    for m in range(rows):
        real = own[m, 0]
        imag = own[m, 1]
        for part in parts[m // per :: rows // per]:
            real = real + part[m % per, 0]
            imag = imag + part[m % per, 1]
        if turn_in:
            real, imag = sandwich(in_left, real, imag, in_right)
        damping = occupation[m, 0].astype(jnp.float32) * decay[0]
        for k in range(1, decay.shape[0]):
            damping = damping + occupation[m, k].astype(jnp.float32) * decay[k]
        real, imag = solved(real, imag, damping, splitting)
        if turn_out:
            real, imag = sandwich(out_left, real, imag, out_right)
        outs[0][m, 0] = real
        outs[0][m, 1] = imag


def turn_kernel(left_ref, right_ref, x, out):
    w_left = as_left(left_ref[...])
    w_right = as_right(right_ref[...])
    for m in range(x.shape[0]):
        real, imag = sandwich(w_left, x[m, 0], x[m, 1], w_right)
        out[m, 0] = real
        out[m, 1] = imag


def turn_one_kernel(left_ref, right_ref, x, out):
    out[...] = left_dot(as_left(left_ref[...]), right_dot(x[...], as_right(right_ref[...])))


def call(kernel, outs, scalars, arrays, scratch=(), products=0, name=None):
    n = arrays[0].shape[-1]
    moved = sum(a.size * 4 for a in arrays) + sum(o.size * 4 for o in outs)
    return pl.pallas_call(
        kernel,
        out_shape=outs,
        in_specs=[pl.BlockSpec(memory_space=SMEM)] * len(scalars)
        + [pl.BlockSpec(memory_space=VMEM)] * len(arrays),
        out_specs=[pl.BlockSpec(memory_space=VMEM)] * len(outs),
        scratch_shapes=scratch,
        compiler_params=pltpu.CompilerParams(vmem_limit_bytes=40 * 1024 * 1024),
        cost_estimate=pl.CostEstimate(
            flops=products * 6 * n**3, bytes_accessed=moved, transcendentals=0
        ),
        name=name,
    )(*scalars, *arrays)


def body(
    tier_four,
    tier_six,
    tier_seven,
    coupling,
    eigenbasis,
    energies,
    decay_rates,
    bath_coefficients,
    occupation_five,
    local_five,
    peers_five,
    places_five,
    occupation_six,
    local_six,
    peers_six,
    places_six,
):
    rows = tier_four.shape[0]
    n = tier_four.shape[-1]
    peer_count = lax.axis_size("mb")
    row_count = lax.axis_size("ma")
    chips = peer_count // 2
    whole = jax.ShapeDtypeStruct(tier_four.shape, jnp.float32)
    piece = jax.ShapeDtypeStruct((rows // HALVES,) + tier_four.shape[1:], jnp.float32)
    pair = [pltpu.VMEM(tier_four.shape[1:], jnp.float32)] * 2

    def table_of(peers, places, occupation):
        return [peers.reshape(-1), places.reshape(-1), occupation[:, 1:3].reshape(-1)]

    mine = jnp.concatenate(
        table_of(peers_five, places_five, occupation_five)
        + table_of(peers_six, places_six, occupation_six)
    )
    table = lax.all_to_all(
        jnp.broadcast_to(mine[None], (peer_count,) + mine.shape),
        "mb",
        split_axis=0,
        concat_axis=0,
        tiled=True,
    )
    columns = (0, mine.shape[0] // 2)

    index = lax.axis_index("mb")
    chip = index // 2
    core = index % 2
    mirrored = chip >= chips // 2
    depth = jnp.where(mirrored, chips - 1 - chip, chip)
    order = jnp.arange(chips, dtype=jnp.int32)
    ahead = chips - 1 - depth
    seen = jnp.where(order < ahead, chips - 1 - order, order - ahead)
    seen = jnp.where(order == chips - 1, depth, seen)
    goal = jnp.where(mirrored, chips - 1 - seen, seen) * 2 + core
    place = jnp.concatenate([chip[None], core[None], goal]).astype(jnp.int32)

    def sibling_of(array):
        return lax.ppermute(array, "mb", [(i, i ^ 1) for i in range(peer_count)])

    def along(array, by):
        return lax.ppermute(
            array, "ma", [(i, (i + by) % row_count) for i in range(row_count)]
        )

    def hop(array, step):
        pairs = []
        for c in range(2):
            pairs.append((step * 2 + c, (step + 1) * 2 + c))
            pairs.append(((chips - 1 - step) * 2 + c, (chips - 2 - step) * 2 + c))
        return lax.ppermute(array, "mb", pairs)

    def reduce_line(tier, upper, lower, c):
        sent = {}
        for slot in range(chips - 1):
            sent[slot] = call(
                functools.partial(partial_kernel, slot, columns[tier]),
                [piece] * HALVES,
                [place, table, bath_coefficients],
                [*upper, *lower, c],
                pair,
                rows * 4,
                f"partial_{tier}_{slot}",
            )
        arrived = {}
        last = []
        for goal_step in range(chips - 1, 0, -1):
            for half in range(HALVES):
                for step in range(goal_step):
                    slot = chips - 1 - goal_step + (step if step >= chips // 2 else 0)
                    message = sent[slot][half]
                    if step > 0:
                        message = message + arrived[step - 1, half]
                    arrived[step, half] = hop(message, step)
                last.append(arrived[goal_step - 1, half])
        return last

    def own_part(tier, upper, lower, raised, lowered, nearby, occupation, c):
        return call(
            functools.partial(own_kernel, chips - 1, columns[tier]),
            [whole],
            [place, table, bath_coefficients, nearby.reshape(rows, -1), occupation],
            [*upper, *lower, raised, lowered, c],
            pair,
            rows * 4,
            f"own_{tier}",
        )[0]

    turned = jnp.transpose(eigenbasis)
    e_row = energies[None, :]
    e_column = energies[:, None]

    def solve(own, last, occupation, turn_in, turn_out, name):
        return call(
            functools.partial(solve_kernel, len(last), turn_in, turn_out),
            [whole],
            [occupation, decay_rates],
            [e_row, e_column, eigenbasis, turned, own, *last],
            (),
            rows * 4,
            name,
        )[0]

    upper_five = (tier_six, sibling_of(tier_six))
    lower_five = (tier_four, sibling_of(tier_four))
    raised_five = along(tier_six, -1)
    lowered_five = along(tier_four, 1)
    last_five = reduce_line(0, upper_five, lower_five, coupling)
    own_five = own_part(
        0, upper_five, lower_five, raised_five, lowered_five, local_five, occupation_five, coupling
    )

    tilted = call(
        turn_one_kernel,
        [jax.ShapeDtypeStruct((n, n), jnp.float32)],
        [],
        [turned, eigenbasis, coupling],
        (),
        2,
        "tilt_coupling",
    )[0]
    eigen_seven = call(
        turn_kernel, [whole], [], [turned, eigenbasis, tier_seven], (), rows * 4, "tilt_seven"
    )[0]
    upper_six = (eigen_seven, sibling_of(eigen_seven))
    raised_six = along(eigen_seven, -1)

    eigen_five = solve(own_five, last_five, occupation_five, True, False, "solve_five")
    lower_six = (eigen_five, sibling_of(eigen_five))
    lowered_six = along(eigen_five, 1)
    last_six = reduce_line(1, upper_six, lower_six, tilted)
    updated_five = call(
        turn_kernel, [whole], [], [eigenbasis, turned, eigen_five], (), rows * 4, "back_five"
    )[0]
    own_six = own_part(
        1, upper_six, lower_six, raised_six, lowered_six, local_six, occupation_six, tilted
    )
    updated_six = solve(own_six, last_six, occupation_six, False, True, "solve_six")
    return (updated_five, updated_six)


def solution(mesh):
    by_block = P(("ma", "mb"))
    in_specs = (by_block,) * 3 + (P(),) * 5 + (by_block,) * 8
    return jax.shard_map(
        body, mesh=mesh, in_specs=in_specs, out_specs=(by_block, by_block), check_vma=False
    )
```

```python
import functools

import jax
import jax.numpy as jnp
from jax import lax
from jax.experimental import pallas as pl
from jax.experimental.pallas import tpu as pltpu
from jax.sharding import PartitionSpec as P

SMEM = pltpu.SMEM
VMEM = pltpu.VMEM
HALVES = 2
TOGETHER = 2


def split(x):
    high = x.astype(jnp.bfloat16)
    return high, (x - high.astype(jnp.float32)).astype(jnp.bfloat16)


def as_left(w):
    high, low = split(w)
    return jnp.concatenate([high, high, low], axis=1)


def as_right(w):
    high, low = split(w)
    return jnp.concatenate([high, high, low], axis=0)


def left_dot(w_left, x):
    high, low = split(x)
    return jnp.dot(
        w_left, jnp.concatenate([high, low, high], axis=0), preferred_element_type=jnp.float32
    )


def right_dot(x, w_right):
    high, low = split(x)
    return jnp.dot(
        jnp.concatenate([high, low, high], axis=1), w_right, preferred_element_type=jnp.float32
    )


def sandwich(w_left, real, imag, w_right):
    n = real.shape[0]
    right = right_dot(jnp.concatenate([real, imag], axis=0), w_right)
    both = left_dot(w_left, jnp.concatenate([right[:n], right[n:]], axis=1))
    return both[:, :n], both[:, n:]


def drive_of(mixed, turned, c_left, c_right):
    n = mixed.shape[-1]
    ahead = left_dot(
        c_left, jnp.concatenate([mixed[1] + turned[0], mixed[0] - turned[1]], axis=1)
    )
    behind = right_dot(
        jnp.concatenate([mixed[1] - turned[0], mixed[0] + turned[1]], axis=0), c_right
    )
    return behind[:n] - ahead[:, :n], ahead[:, n:] - behind[n:]


def add_requests(row, column, place, table, bath, upper, lower, mixed, turned):
    chip = place[0]
    core = place[1]
    for j in range(4):
        peer = table[row, column + j]
        spot = table[row, column + 4 + j]
        here = peer >> 1 == chip
        for sibling in range(2):
            own = (peer & 1 == core) if sibling == 0 else (peer & 1 != core)

            @pl.when(jnp.logical_and(here, own))
            def _(j=j, sibling=sibling, spot=spot):
                if j < 2:
                    mixed[...] += upper[sibling][spot]
                else:
                    mode = j - 1
                    count = table[row, column + 6 + j].astype(jnp.float32)
                    source = lower[sibling][spot]
                    mixed[...] += (count * bath[0, mode]) * source
                    turned[...] += (count * bath[1, mode]) * source


def joined(pieces, scratch):
    if len(pieces) == 1:
        return pieces[0]
    row = 0
    for piece in pieces:
        scratch[row : row + piece.shape[0]] = piece[...]
        row += piece.shape[0]
    return scratch


def partial_kernel(slot, first, column, role, place, table, bath, *refs):
    upper, pieces, (c_ref, out, mixed, turned, sibling) = refs[:2], refs[3:-5], refs[-5:]
    rows = upper[0].shape[0]
    together = mixed.shape[0]

    def work():
        c_left = as_left(c_ref[...])
        c_right = as_right(c_ref[...])
        lower = (refs[2], joined(pieces, sibling))

        @pl.loop(0, out.shape[0], step=together)
        def _(m):
            mixed[...] = jnp.zeros_like(mixed)
            turned[...] = jnp.zeros_like(turned)
            for u in range(together):
                add_requests(
                    place[3 + slot] * rows + first + m + u,
                    column,
                    place,
                    table,
                    bath,
                    upper,
                    lower,
                    mixed.at[u],
                    turned.at[u],
                )
            for u in range(together):
                real, imag = drive_of(mixed[u], turned[u], c_left, c_right)
                out[m + u, 0] = real
                out[m + u, 1] = imag

    by_role(role, place, work)


def by_role(role, place, work):
    if role == "all":
        work()
    elif role == "ends":
        pl.when(place[2] == 0)(work)
    else:
        pl.when(place[2] != 0)(work)


def sums_kernel(slot, column, place, table, bath, nearby, occupation, *refs):
    upper, pieces, (mixed_out, turned_out, sibling) = refs[:2], refs[3:-3], refs[-3:]
    lower = (refs[2], joined(pieces, sibling))
    rows = upper[0].shape[0]
    modes = bath.shape[1]

    @pl.loop(0, rows)
    def _(m):
        mixed = mixed_out.at[m]
        turned = turned_out.at[m]
        mixed[...] = upper[0][nearby[m, 0]]
        turned[...] = jnp.zeros_like(turned)
        add_requests(
            place[3 + slot] * rows + m, column, place, table, bath, upper, lower, mixed, turned
        )
        for k in range(3, modes):
            if k > 3:
                mixed[...] += upper[0][nearby[m, k - 3]]
            held = occupation[m, k]

            @pl.when(held > 0)
            def _(k=k, held=held):
                source = lower[0][nearby[m, modes - 3 + k - 3]]
                mixed[...] += (held.astype(jnp.float32) * bath[0, k]) * source
                turned[...] += (held.astype(jnp.float32) * bath[1, k]) * source


def own_drive(m, occupation, bath, mixed, turned, raised, lowered, c_left, c_right):
    count = occupation[m, 0].astype(jnp.float32)
    below = lowered[m]
    return drive_of(
        mixed[m] + raised[m] + (count * bath[0, 0]) * below,
        turned[m] + (count * bath[1, 0]) * below,
        c_left,
        c_right,
    )


def finish_kernel(occupation, bath, c_ref, mixed, turned, raised, lowered, out):
    c_left = as_left(c_ref[...])
    c_right = as_right(c_ref[...])
    for m in range(out.shape[0]):
        real, imag = own_drive(
            m, occupation, bath, mixed, turned, raised, lowered, c_left, c_right
        )
        out[m, 0] = real
        out[m, 1] = imag


def solved(real, imag, damping, splitting):
    inverse = 1.0 / (damping * damping + splitting * splitting)
    factor_real = -damping * inverse
    factor_imag = splitting * inverse
    return real * factor_real - imag * factor_imag, real * factor_imag + imag * factor_real


def damping_of(occupation, decay, m):
    damping = occupation[m, 0].astype(jnp.float32) * decay[0]
    for k in range(1, decay.shape[0]):
        damping = damping + occupation[m, k].astype(jnp.float32) * decay[k]
    return damping


def solve_five_kernel(
    counts, role, place, occupation, decay, bath, e_row, e_column, e_ref, et_ref, c_ref, *rest
):
    mixed, turned, raised, lowered = rest[:4]
    rest = rest[4:]
    arrivals = []
    for count in counts[1:]:
        arrivals.append(rows_of(rest[:count]))
        rest = rest[count:]
    previous, (out, *pieces) = rest[: counts[0]], rest[counts[0] :]
    spots = rows_of(pieces)

    def work():
        splitting = e_column[...] - e_row[...]
        in_left = as_left(et_ref[...])
        in_right = as_right(e_ref[...])
        c_left = as_left(c_ref[...])
        c_right = as_right(c_ref[...])
        for m in range(out.shape[0]):
            real, imag = own_drive(
                m, occupation, bath, mixed, turned, raised, lowered, c_left, c_right
            )
            for arrival in arrivals:
                piece, row = arrival[m]
                real = real + piece[row, 0]
                imag = imag + piece[row, 1]
            real, imag = sandwich(in_left, real, imag, in_right)
            damping = damping_of(occupation, decay, m)
            real, imag = solved(real, imag, damping, splitting)
            out[m, 0] = real
            out[m, 1] = imag
            piece, row = spots[m]
            piece[row, 0] = real
            piece[row, 1] = imag

    by_role(role, place, work)
    if role == "rest":

        @pl.when(place[2] == 0)
        def _():
            out[...] = previous[0][...]
            first = 0
            for piece in pieces:
                piece[...] = previous[0][first : first + piece.shape[0]]
                first += piece.shape[0]


def solve_six_kernel(
    first, part_count, occupation, decay, e_row, e_column, e_ref, et_ref, own, *rest
):
    parts, out = rest[:part_count], rest[-1]
    splitting = e_column[...] - e_row[...]
    out_left = as_left(e_ref[...])
    out_right = as_right(et_ref[...])
    for m in range(out.shape[0]):
        real = own[m, 0]
        imag = own[m, 1]
        for part in parts:
            real = real + part[m, 0]
            imag = imag + part[m, 1]
        damping = damping_of(occupation, decay, first + m)
        real, imag = solved(real, imag, damping, splitting)
        real, imag = sandwich(out_left, real, imag, out_right)
        out[m, 0] = real
        out[m, 1] = imag


def turn_kernel(left_ref, right_ref, x, *outs):
    w_left = as_left(left_ref[...])
    w_right = as_right(right_ref[...])
    spots = [rows_of(outs[:1]), rows_of(outs[1:])] if len(outs) > 1 else [rows_of(outs)]
    for m in range(x.shape[0]):
        real, imag = sandwich(w_left, x[m, 0], x[m, 1], w_right)
        for spot in spots:
            out, row = spot[m]
            out[row, 0] = real
            out[row, 1] = imag


def turn_one_kernel(left_ref, right_ref, x, out):
    out[...] = left_dot(as_left(left_ref[...]), right_dot(x[...], as_right(right_ref[...])))


def rows_of(pieces):
    return [(piece, row) for piece in pieces for row in range(piece.shape[0])]


def add_kernel(counts, *refs):
    ours, theirs, outs = refs[: counts[0]], refs[counts[0] : sum(counts)], refs[sum(counts) :]
    for (a, i), (b, j), (out, k) in zip(rows_of(ours), rows_of(theirs), rows_of(outs)):
        out[k] = a[i] + b[j]


class Queue:
    def __init__(self):
        self.latest = []

    def call(
        self, kernel, outs, scalars, arrays, scratch=(), name=None, in_specs=None, after=(), **options
    ):
        waits = [w for w in [*self.latest, *after] if not any(w is a for a in arrays)]
        plain = pl.BlockSpec(memory_space=VMEM)
        count = len(scalars) + len(arrays)

        def without_waits(*refs):
            kernel(*refs[:count], *refs[count + len(waits) :])

        got = pl.pallas_call(
            without_waits,
            out_shape=outs,
            in_specs=[pl.BlockSpec(memory_space=SMEM)] * len(scalars)
            + (in_specs or [plain] * len(arrays))
            + [pl.BlockSpec(memory_space=pl.ANY)] * len(waits),
            out_specs=options.pop("out_specs", [plain] * len(outs)),
            scratch_shapes=scratch,
            compiler_params=pltpu.CompilerParams(vmem_limit_bytes=24 * 1024 * 1024),
            cost_estimate=pl.CostEstimate(flops=1, bytes_accessed=1, transcendentals=0),
            name=name,
            **options,
        )(*scalars, *arrays, *waits)
        self.latest = [got[0]]
        return got


def body(
    tier_four,
    tier_six,
    tier_seven,
    coupling,
    eigenbasis,
    energies,
    decay_rates,
    bath_coefficients,
    occupation_five,
    local_five,
    peers_five,
    places_five,
    occupation_six,
    local_six,
    peers_six,
    places_six,
):
    queue = Queue()
    call = queue.call
    rows = tier_four.shape[0]
    n = tier_four.shape[-1]
    peer_count = lax.axis_size("mb")
    row_count = lax.axis_size("ma")
    chips = peer_count // 2
    per = rows // HALVES
    whole = jax.ShapeDtypeStruct(tier_four.shape, jnp.float32)
    a_tier = pltpu.VMEM(tier_four.shape, jnp.float32)
    work_space = [pltpu.VMEM((TOGETHER,) + tier_four.shape[1:], jnp.float32)] * 2 + [a_tier]

    def sibling_of(array, of_chips):
        return lax.ppermute(
            array, "mb", [(2 * i + c, 2 * i + 1 - c) for i in of_chips for c in range(2)]
        )

    def along(array, by):
        return lax.ppermute(array, "ma", [(i, (i + by) % row_count) for i in range(row_count)])

    def turn_line(array, by):
        return lax.ppermute(
            array, "mb", [(i, (i + 2 * by) % peer_count) for i in range(peer_count)]
        )

    def hop(array, *moves):
        pairs = []
        for start, stop in moves:
            for c in range(2):
                pairs.append((start * 2 + c, stop * 2 + c))
                pairs.append(((chips - 1 - start) * 2 + c, (chips - 1 - stop) * 2 + c))
        return lax.ppermute(array, "mb", pairs)

    mine = jnp.concatenate(
        [
            peers_five,
            places_five,
            occupation_five[:, 1:3],
            peers_six,
            places_six,
            occupation_six[:, 1:3],
        ],
        axis=1,
    )
    table = jnp.concatenate([mine] + [turn_line(mine, by) for by in range(1, chips)], axis=0)
    columns = (0, mine.shape[1] // 2)

    goals = list(range(chips - 1, 0, -1))
    skips = chips > 3

    def slot_of(step, g):
        depth = min(step, chips - 1 - step)
        behind = step >= chips // 2
        return chips - 1 - g if behind else depth + chips - 1 - g

    index = lax.axis_index("mb")
    chip = index // 2
    mirrored = chip >= chips // 2
    depth = jnp.where(mirrored, chips - 1 - chip, chip)
    order = jnp.arange(chips, dtype=jnp.int32)
    seen = jnp.where(order < depth, order, chips - 1 - order + depth)
    goal = jnp.where(mirrored, chips - 1 - seen, seen)
    place = jnp.concatenate(
        [jnp.stack([chip, index % 2, depth]), (chip - goal + chips) % chips]
    ).astype(jnp.int32)

    def partial(tier, slot, upper, lower, c, role, after=(), half=None):
        first, count = (0, rows) if half is None else (half * per, per)
        return call(
            functools.partial(partial_kernel, slot, first, columns[tier], role),
            [jax.ShapeDtypeStruct((count,) + whole.shape[1:], jnp.float32)],
            [place, table, bath_coefficients],
            [*upper, *lower, c],
            work_space,
            f"partial_{tier}_{slot}_{first}_{role}",
            after=after,
        )[0]

    def steps_to(g):
        last = g - 1 if skips and g == chips - 1 else g
        return list(range(last))

    def next_stop(step, g):
        return g if step == steps_to(g)[-1] else step + 1

    def start(sent, g):
        return [hop(array, (0, next_stop(0, g))) for array in sent[slot_of(0, g)]]

    def go_on(tier, sent, arrived, g, after=(), count=1):
        for step in steps_to(g)[1:]:
            parts = count if step == steps_to(g)[-1] else 1
            ours = sent[slot_of(step, g)]
            piece = jax.ShapeDtypeStruct((rows // parts,) + whole.shape[1:], jnp.float32)
            messages = call(
                functools.partial(add_kernel, (len(ours), len(arrived))),
                [piece] * parts,
                [],
                [*ours, *arrived],
                (),
                f"add_{tier}_{step}_{g}",
                after=after,
            )
            arrived = [hop(message, (step, next_stop(step, g))) for message in messages]
        return arrived

    def sums(tier, upper, lower, nearby, occupation):
        return call(
            functools.partial(sums_kernel, chips - 1, columns[tier]),
            [whole, whole],
            [place, table, bath_coefficients, nearby.reshape(rows, -1), occupation],
            [*upper, *lower],
            [a_tier],
            f"sums_{tier}",
        )

    turned = jnp.transpose(eigenbasis)
    bases = [energies[None, :], energies[:, None], eigenbasis, turned]
    every = range(chips)
    ends = [0, chips - 1]

    def solve_five(arrays, last, role, previous, cuts, after=()):
        got = call(
            functools.partial(
                solve_five_kernel, [len(previous), *[len(pieces) for pieces in last]], role
            ),
            [whole]
            + [jax.ShapeDtypeStruct((cut,) + whole.shape[1:], jnp.float32) for cut in cuts],
            [place, occupation_five, decay_rates, bath_coefficients],
            [*bases, coupling, *arrays, *[piece for pieces in last for piece in pieces], *previous],
            (),
            f"solve_five_{role}",
            after=after,
        )
        return got[0], got[1:]

    def solve_six(own, last, half, previous):
        plain = pl.BlockSpec(memory_space=VMEM)
        block = pl.BlockSpec((per,) + whole.shape[1:], lambda i: (half, 0, 0, 0))
        parts = [pieces[half * len(pieces) // HALVES] for pieces in last]
        arrays = [*bases, own, *parts, *previous]
        return call(
            functools.partial(solve_six_kernel, half * per, len(parts)),
            [whole],
            [occupation_six, decay_rates],
            arrays,
            (),
            f"solve_six_{half}",
            [plain] * len(bases)
            + [block]
            + [block if len(pieces) == 1 else plain for pieces in last]
            + [pl.BlockSpec(memory_space=pl.ANY)] * len(previous),
            out_specs=[block],
            grid=(1,),
            input_output_aliases={2 + len(arrays) - 1: 0} if previous else {},
        )

    raised_five = along(tier_six, -1)
    lowered_five = along(tier_four, 1)
    upper_five = (tier_six, sibling_of(tier_six, every))
    lower_five = (tier_four, sibling_of(tier_four, every))
    slots = range(chips - 1)
    far = goals[0]
    aside = [(far - 1, far)] if skips else []
    sent_five = {}
    moving_five = {}
    sent_five[0] = [
        partial(0, 0, upper_five, lower_five, coupling, "all", (), half) for half in range(HALVES)
    ]
    moving_five[far] = [hop(array, (0, next_stop(0, far)), *aside) for array in sent_five[0]]
    beside_five = [moving_five[far]] if skips else []
    for slot in slots[1:]:
        sent_five[slot] = [partial(0, slot, upper_five, lower_five, coupling, "all")]
        moving_five[goals[slot]] = start(sent_five, goals[slot])
    sums_five = sums(0, upper_five, lower_five, local_five, occupation_five)
    tilted = call(
        turn_one_kernel,
        [jax.ShapeDtypeStruct((n, n), jnp.float32)],
        [],
        [turned, eigenbasis, coupling],
        (),
        "tilt_coupling",
    )[0]
    moving_five[far] = go_on(0, sent_five, moving_five[far], far)
    eigen_seven, *pieces = call(
        turn_kernel,
        [whole] + [jax.ShapeDtypeStruct((per,) + whole.shape[1:], jnp.float32)] * HALVES,
        [],
        [turned, eigenbasis, tier_seven],
        (),
        "tilt_seven",
        after=[raised_five],
    )
    pieces = [sibling_of(piece, every) for piece in pieces]
    upper_six = (eigen_seven, jnp.concatenate(pieces))
    raised_six = along(eigen_seven, -1)
    for g in goals[1:]:
        after = [lowered_five, *pieces] if g == goals[-2] else []
        moving_five[g] = go_on(0, sent_five, moving_five[g], g, after)
    own_five = [*sums_five, raised_five, lowered_five]
    last = [moving_five[far], *beside_five]
    ends_five, pieces = solve_five(own_five, last, "ends", [], [per] * HALVES)
    lower_ends = (ends_five, *[sibling_of(piece, ends) for piece in pieces])
    sent_ends = {}
    moving_six = {}

    def from_ends(slot, after=()):
        sent_ends[slot] = [partial(1, slot, upper_six, lower_ends, tilted, "ends", after)]
        moving_six[goals[slot]] = start(sent_ends, goals[slot])

    from_ends(0, moving_five[goals[-1]])
    for slot in slots[1:]:
        from_ends(slot)
    last = [moving_five[g] for g in goals[1:]]
    cuts = [rows - rows // 4, rows // 4]
    eigen_five, pieces = solve_five(own_five, last, "rest", [ends_five], cuts, [raised_six])
    lower_six = (eigen_five, *[sibling_of(piece, every) for piece in pieces])
    lowered_six = along(eigen_five, 1)
    sent_six = {}

    def from_rest(slot):
        if slot not in sent_six:
            sent_six[slot] = [partial(1, slot, upper_six, lower_six, tilted, "rest")]

    from_rest(0)
    beside_six = [hop(sent_six[0][0], *aside)] if skips else []
    for step in steps_to(far)[1:]:
        from_rest(slot_of(step, far))
    moving_six[far] = go_on(1, sent_six, moving_six[far], far)
    for slot in slots:
        from_rest(slot)
    sums_six = sums(1, upper_six, lower_six, local_six, occupation_six)
    for g in goals[1:]:
        moving_six[g] = go_on(1, sent_six, moving_six[g], g, [], HALVES)
    updated_five = call(
        turn_kernel, [whole], [], [eigenbasis, turned, eigen_five], (), "back_five"
    )[0]
    own_six = call(
        finish_kernel,
        [whole],
        [occupation_six, bath_coefficients],
        [tilted, *sums_six, raised_six, lowered_six],
        (),
        "finish_six",
    )[0]
    previous = []
    for half in range(HALVES):
        last = [moving_six[g] for g in goals[1:]]
        last += [moving_six[far], *[[array] for array in beside_six]]
        previous = solve_six(own_six, last, half, previous)
    return (updated_five, previous[0])


def solution(mesh):
    by_block = P(("ma", "mb"))
    in_specs = (by_block,) * 3 + (P(),) * 5 + (by_block,) * 8
    return jax.shard_map(
        body, mesh=mesh, in_specs=in_specs, out_specs=(by_block, by_block), check_vma=False
    )
```

```python
import functools
import math

import jax
import jax.numpy as jnp
from jax import lax
from jax.experimental import pallas as pl
from jax.experimental.pallas import tpu as pltpu
from jax.sharding import PartitionSpec as P

SMEM = pltpu.SMEM
VMEM = pltpu.VMEM
HALVES = 2
TOGETHER = 4


def split(x):
    high = x.astype(jnp.bfloat16)
    return high, (x - high.astype(jnp.float32)).astype(jnp.bfloat16)


def as_left(w):
    high, low = split(w)
    return jnp.concatenate([high, high, low], axis=1)


def as_right(w):
    high, low = split(w)
    return jnp.concatenate([high, high, low], axis=0)


def left_dot(w_left, x):
    high, low = split(x)
    return jnp.dot(
        w_left, jnp.concatenate([high, low, high], axis=0), preferred_element_type=jnp.float32
    )


def right_dot(x, w_right):
    high, low = split(x)
    return jnp.dot(
        jnp.concatenate([high, low, high], axis=1), w_right, preferred_element_type=jnp.float32
    )


def sandwich(w_left, real, imag, w_right):
    n = real.shape[0]
    right = right_dot(jnp.concatenate([real, imag], axis=0), w_right)
    both = left_dot(w_left, jnp.concatenate([right[:n], right[n:]], axis=1))
    return both[:, :n], both[:, n:]


def drive_of(mixed, turned, c_left, c_right):
    n = mixed.shape[-1]
    ahead = left_dot(
        c_left, jnp.concatenate([mixed[1] + turned[0], mixed[0] - turned[1]], axis=1)
    )
    behind = right_dot(
        jnp.concatenate([mixed[1] - turned[0], mixed[0] + turned[1]], axis=0), c_right
    )
    return behind[:n] - ahead[:, :n], ahead[:, n:] - behind[n:]


def add_requests(row, column, place, table, bath, upper, lower, mixed, turned):
    chip = place[0]
    core = place[1]
    for j in range(4):
        peer = table[row, column + j]
        spot = table[row, column + 4 + j]
        here = peer >> 1 == chip
        own, *pieces = upper if j < 2 else lower
        first = 0
        for number, source in enumerate([own, *pieces]):
            if number == 0:
                held = jnp.logical_and(here, peer & 1 == core)
                at = spot
            else:
                held = jnp.logical_and(here, peer & 1 != core)
                if len(pieces) > 1:
                    inside = jnp.logical_and(spot >= first, spot < first + source.shape[0])
                    held = jnp.logical_and(held, inside)
                at = spot - first
                first += source.shape[0]

            @pl.when(held)
            def _(j=j, source=source, at=at):
                if j < 2:
                    mixed[...] += source[at]
                else:
                    mode = j - 1
                    count = table[row, column + 6 + j].astype(jnp.float32)
                    mixed[...] += (count * bath[0, mode]) * source[at]
                    turned[...] += (count * bath[1, mode]) * source[at]


def partial_kernel(slot, column, role, counts, place, table, bath, *refs):
    upper, lower = refs[: counts[0]], refs[counts[0] : sum(counts)]
    c_ref, out, mixed, turned = refs[sum(counts) :]
    rows = upper[0].shape[0]
    together = mixed.shape[0]

    def work():
        c_left = as_left(c_ref[...])
        c_right = as_right(c_ref[...])

        @pl.loop(0, out.shape[0], step=together)
        def _(m):
            mixed[...] = jnp.zeros_like(mixed)
            turned[...] = jnp.zeros_like(turned)
            for u in range(together):
                add_requests(
                    place[3 + slot] * rows + m + u,
                    column,
                    place,
                    table,
                    bath,
                    upper,
                    lower,
                    mixed.at[u],
                    turned.at[u],
                )
            for u in range(together):
                real, imag = drive_of(mixed[u], turned[u], c_left, c_right)
                out[m + u, 0] = real
                out[m + u, 1] = imag

    by_role(role, place, work)


def by_role(role, place, work):
    if role == "all":
        work()
    elif role == "ends":
        pl.when(place[2] == 0)(work)
    else:
        pl.when(place[2] != 0)(work)


def sums_kernel(slot, column, counts, place, table, bath, nearby, occupation, *refs):
    upper, lower = refs[: counts[0]], refs[counts[0] : sum(counts)]
    mixed_out, turned_out = refs[sum(counts) :]
    rows = upper[0].shape[0]
    modes = bath.shape[1]

    @pl.loop(0, rows)
    def _(m):
        mixed = mixed_out.at[m]
        turned = turned_out.at[m]
        mixed[...] = upper[0][nearby[m, 0]]
        turned[...] = jnp.zeros_like(turned)
        add_requests(
            place[3 + slot] * rows + m, column, place, table, bath, upper, lower, mixed, turned
        )
        for k in range(3, modes):
            if k > 3:
                mixed[...] += upper[0][nearby[m, k - 3]]
            held = occupation[m, k]

            @pl.when(held > 0)
            def _(k=k, held=held):
                source = lower[0][nearby[m, modes - 3 + k - 3]]
                mixed[...] += (held.astype(jnp.float32) * bath[0, k]) * source
                turned[...] += (held.astype(jnp.float32) * bath[1, k]) * source


def own_drive(m, occupation, bath, mixed, turned, raised, lowered, c_left, c_right):
    count = occupation[m, 0].astype(jnp.float32)
    below = lowered[m]
    return drive_of(
        mixed[m] + raised[m] + (count * bath[0, 0]) * below,
        turned[m] + (count * bath[1, 0]) * below,
        c_left,
        c_right,
    )


def finish_kernel(occupation, bath, c_ref, mixed, turned, raised, lowered, out):
    c_left = as_left(c_ref[...])
    c_right = as_right(c_ref[...])
    for m in range(out.shape[0]):
        real, imag = own_drive(
            m, occupation, bath, mixed, turned, raised, lowered, c_left, c_right
        )
        out[m, 0] = real
        out[m, 1] = imag


def solved(real, imag, damping, splitting):
    inverse = 1.0 / (damping * damping + splitting * splitting)
    factor_real = -damping * inverse
    factor_imag = splitting * inverse
    return real * factor_real - imag * factor_imag, real * factor_imag + imag * factor_real


def damping_of(occupation, decay, m):
    damping = occupation[m, 0].astype(jnp.float32) * decay[0]
    for k in range(1, decay.shape[0]):
        damping = damping + occupation[m, k].astype(jnp.float32) * decay[k]
    return damping


def solve_five_kernel(
    counts, role, place, occupation, decay, e_row, e_column, e_ref, et_ref, own, *rest
):
    arrivals = []
    for count in counts[1:]:
        arrivals.append(rows_of(rest[:count]))
        rest = rest[count:]
    previous, (out, *pieces) = rest[: counts[0]], rest[counts[0] :]
    spots = rows_of(pieces)

    def work():
        splitting = e_column[...] - e_row[...]
        in_left = as_left(et_ref[...])
        in_right = as_right(e_ref[...])
        for m in range(out.shape[0]):
            real = own[m, 0]
            imag = own[m, 1]
            for arrival in arrivals:
                piece, row = arrival[m]
                real = real + piece[row, 0]
                imag = imag + piece[row, 1]
            real, imag = sandwich(in_left, real, imag, in_right)
            damping = damping_of(occupation, decay, m)
            real, imag = solved(real, imag, damping, splitting)
            out[m, 0] = real
            out[m, 1] = imag
            piece, row = spots[m]
            piece[row, 0] = real
            piece[row, 1] = imag

    by_role(role, place, work)
    if role == "rest":

        @pl.when(place[2] == 0)
        def _():
            out[...] = previous[0][...]
            first = 0
            for piece in pieces:
                piece[...] = previous[0][first : first + piece.shape[0]]
                first += piece.shape[0]


def solve_six_kernel(
    first, part_count, occupation, decay, e_row, e_column, e_ref, et_ref, own, *rest
):
    parts, out = rest[:part_count], rest[-1]
    splitting = e_column[...] - e_row[...]
    out_left = as_left(e_ref[...])
    out_right = as_right(et_ref[...])
    for m in range(out.shape[0]):
        real = own[m, 0]
        imag = own[m, 1]
        for part in parts:
            real = real + part[m, 0]
            imag = imag + part[m, 1]
        damping = damping_of(occupation, decay, first + m)
        real, imag = solved(real, imag, damping, splitting)
        real, imag = sandwich(out_left, real, imag, out_right)
        out[m, 0] = real
        out[m, 1] = imag


def turn_kernel(left_ref, right_ref, x, *outs):
    w_left = as_left(left_ref[...])
    w_right = as_right(right_ref[...])
    spots = [rows_of(outs[:1]), rows_of(outs[1:])] if len(outs) > 1 else [rows_of(outs)]
    for m in range(x.shape[0]):
        real, imag = sandwich(w_left, x[m, 0], x[m, 1], w_right)
        for spot in spots:
            out, row = spot[m]
            out[row, 0] = real
            out[row, 1] = imag


def turn_one_kernel(left_ref, right_ref, x, out):
    out[...] = left_dot(as_left(left_ref[...]), right_dot(x[...], as_right(right_ref[...])))


def rows_of(pieces):
    return [(piece, row) for piece in pieces for row in range(piece.shape[0])]


def add_kernel(counts, *refs):
    ours, theirs, outs = refs[: counts[0]], refs[counts[0] : sum(counts)], refs[sum(counts) :]
    for (a, i), (b, j), (out, k) in zip(rows_of(ours), rows_of(theirs), rows_of(outs)):
        out[k] = a[i] + b[j]


class Queue:
    def __init__(self):
        self.latest = []

    def call(
        self, kernel, outs, scalars, arrays, scratch=(), name=None, in_specs=None, after=(), **options
    ):
        waits = [w for w in [*self.latest, *after] if not any(w is a for a in arrays)]
        plain = pl.BlockSpec(memory_space=VMEM)
        count = len(scalars) + len(arrays)

        def without_waits(*refs):
            kernel(*refs[:count], *refs[count + len(waits) :])

        got = pl.pallas_call(
            without_waits,
            out_shape=outs,
            in_specs=[pl.BlockSpec(memory_space=SMEM)] * len(scalars)
            + (in_specs or [plain] * len(arrays))
            + [pl.BlockSpec(memory_space=pl.ANY)] * len(waits),
            out_specs=options.pop("out_specs", [plain] * len(outs)),
            scratch_shapes=scratch,
            compiler_params=pltpu.CompilerParams(vmem_limit_bytes=12 * 1024 * 1024),
            cost_estimate=pl.CostEstimate(flops=1, bytes_accessed=1, transcendentals=0),
            name=name,
            **options,
        )(*scalars, *arrays, *waits)
        self.latest = [got[0]]
        return got


def body(
    tier_four,
    tier_six,
    tier_seven,
    coupling,
    eigenbasis,
    energies,
    decay_rates,
    bath_coefficients,
    occupation_five,
    local_five,
    peers_five,
    places_five,
    occupation_six,
    local_six,
    peers_six,
    places_six,
):
    queue = Queue()
    call = queue.call
    rows = tier_four.shape[0]
    n = tier_four.shape[-1]
    peer_count = lax.axis_size("mb")
    row_count = lax.axis_size("ma")
    chips = peer_count // 2
    per = rows // HALVES
    whole = jax.ShapeDtypeStruct(tier_four.shape, jnp.float32)
    together = math.gcd(rows, TOGETHER)
    work_space = [pltpu.VMEM((together,) + tier_four.shape[1:], jnp.float32)] * 2

    def sibling_of(array, of_chips):
        return lax.ppermute(
            array, "mb", [(2 * i + c, 2 * i + 1 - c) for i in of_chips for c in range(2)]
        )

    def along(array, by):
        return lax.ppermute(array, "ma", [(i, (i + by) % row_count) for i in range(row_count)])

    def turn_line(array, by):
        return lax.ppermute(
            array, "mb", [(i, (i + 2 * by) % peer_count) for i in range(peer_count)]
        )

    def hop(array, *moves):
        pairs = []
        for start, stop in moves:
            for c in range(2):
                pairs.append((start * 2 + c, stop * 2 + c))
                pairs.append(((chips - 1 - start) * 2 + c, (chips - 1 - stop) * 2 + c))
        return lax.ppermute(array, "mb", pairs)

    mine = jnp.concatenate(
        [
            peers_five,
            places_five,
            occupation_five[:, 1:3],
            peers_six,
            places_six,
            occupation_six[:, 1:3],
        ],
        axis=1,
    )
    tables = [mine] + [turn_line(mine, by) for by in range(1, chips)]
    table = jnp.concatenate(tables, axis=0)
    columns = (0, mine.shape[1] // 2)

    goals = list(range(chips - 1, 0, -1))
    skips = chips > 3

    def slot_of(step, g):
        depth = min(step, chips - 1 - step)
        behind = step >= chips // 2
        return chips - 1 - g if behind else depth + chips - 1 - g

    index = lax.axis_index("mb")
    chip = index // 2
    mirrored = chip >= chips // 2
    depth = jnp.where(mirrored, chips - 1 - chip, chip)
    order = jnp.arange(chips, dtype=jnp.int32)
    seen = jnp.where(order < depth, order, chips - 1 - order + depth)
    goal = jnp.where(mirrored, chips - 1 - seen, seen)
    place = jnp.concatenate(
        [jnp.stack([chip, index % 2, depth]), (chip - goal + chips) % chips]
    ).astype(jnp.int32)

    def partial(tier, slot, upper, lower, c, role, after=()):
        return call(
            functools.partial(
                partial_kernel, slot, columns[tier], role, (len(upper), len(lower))
            ),
            [whole],
            [place, table, bath_coefficients],
            [*upper, *lower, c],
            work_space,
            f"partial_{tier}_{slot}_{role}",
            after=after,
        )

    def steps_to(g):
        last = g - 1 if skips and g == chips - 1 else g
        return list(range(last))

    def next_stop(step, g):
        return g if step == steps_to(g)[-1] else step + 1

    def start(sent, g):
        return [hop(array, (0, next_stop(0, g))) for array in sent[slot_of(0, g)]]

    def go_on(tier, sent, arrived, g, after=(), cuts=None):
        for step in steps_to(g)[1:]:
            parts = cuts if cuts and step == steps_to(g)[-1] else [rows]
            ours = sent[slot_of(step, g)]
            messages = call(
                functools.partial(add_kernel, (len(ours), len(arrived))),
                [jax.ShapeDtypeStruct((cut,) + whole.shape[1:], jnp.float32) for cut in parts],
                [],
                [*ours, *arrived],
                (),
                f"add_{tier}_{step}_{g}",
                after=after,
            )
            arrived = [hop(message, (step, next_stop(step, g))) for message in messages]
        return arrived

    def sums(tier, upper, lower, nearby, occupation):
        return call(
            functools.partial(sums_kernel, chips - 1, columns[tier], (len(upper), len(lower))),
            [whole, whole],
            [place, table, bath_coefficients, nearby.reshape(rows, -1), occupation],
            [*upper, *lower],
            (),
            f"sums_{tier}",
        )

    turned = jnp.transpose(eigenbasis)
    bases = [energies[None, :], energies[:, None], eigenbasis, turned]
    every = range(chips)
    ends = [0, chips - 1]

    def solve_five(own, last, role, previous, cuts, after=()):
        got = call(
            functools.partial(
                solve_five_kernel, [len(previous), *[len(pieces) for pieces in last]], role
            ),
            [whole]
            + [jax.ShapeDtypeStruct((cut,) + whole.shape[1:], jnp.float32) for cut in cuts],
            [place, occupation_five, decay_rates],
            [*bases, own, *[piece for pieces in last for piece in pieces], *previous],
            (),
            f"solve_five_{role}",
            after=after,
        )
        return got[0], got[1:]

    last_cuts = [rows - rows // 4, rows // 4]

    def solve_six(own, last, number, previous):
        cut = last_cuts[number]
        plain = pl.BlockSpec(memory_space=VMEM)
        first = sum(last_cuts[:number])
        block = pl.BlockSpec((cut,) + whole.shape[1:], lambda i: (first // cut, 0, 0, 0))
        parts = [pieces[number % len(pieces)] for pieces in last]
        arrays = [*bases, own, *parts, *previous]
        return call(
            functools.partial(solve_six_kernel, first, len(parts)),
            [whole],
            [occupation_six, decay_rates],
            arrays,
            (),
            f"solve_six_{number}",
            [plain] * len(bases)
            + [block]
            + [block if len(pieces) == 1 else plain for pieces in last]
            + [pl.BlockSpec(memory_space=pl.ANY)] * len(previous),
            out_specs=[block],
            grid=(1,),
            input_output_aliases={2 + len(arrays) - 1: 0} if previous else {},
        )

    raised_five = along(tier_six, -1)
    lowered_five = along(tier_four, 1)
    upper_five = (tier_six, sibling_of(tier_six, every))
    lower_five = (tier_four, sibling_of(tier_four, every))
    slots = range(chips - 1)
    far = goals[0]
    aside = [(far - 1, far)] if skips else []
    sent_five = {}
    moving_five = {}
    sent_five[0] = partial(0, 0, upper_five, lower_five, coupling, "all")
    moving_five[far] = [hop(array, (0, next_stop(0, far)), *aside) for array in sent_five[0]]
    beside_five = [moving_five[far]] if skips else []
    for slot in slots[1:]:
        sent_five[slot] = partial(0, slot, upper_five, lower_five, coupling, "all")
        moving_five[goals[slot]] = start(sent_five, goals[slot])
    sums_five = sums(0, upper_five, lower_five, local_five, occupation_five)
    tilted = call(
        turn_one_kernel,
        [jax.ShapeDtypeStruct((n, n), jnp.float32)],
        [],
        [turned, eigenbasis, coupling],
        (),
        "tilt_coupling",
    )[0]
    moving_five[far] = go_on(0, sent_five, moving_five[far], far)
    eigen_seven, *pieces = call(
        turn_kernel,
        [whole] + [jax.ShapeDtypeStruct((per,) + whole.shape[1:], jnp.float32)] * HALVES,
        [],
        [turned, eigenbasis, tier_seven],
        (),
        "tilt_seven",
        after=[raised_five],
    )
    pieces = [sibling_of(piece, every) for piece in pieces]
    upper_six = (eigen_seven, *pieces)
    raised_six = along(eigen_seven, -1)
    for g in goals[1:]:
        after = [lowered_five] if g == goals[-2] else []
        moving_five[g] = go_on(0, sent_five, moving_five[g], g, after)
    own_five = call(
        finish_kernel,
        [whole],
        [occupation_five, bath_coefficients],
        [coupling, *sums_five, raised_five, lowered_five],
        (),
        "finish_five",
        after=pieces,
    )[0]
    last = [moving_five[far], *beside_five]
    ends_five, pieces = solve_five(own_five, last, "ends", [], [per] * HALVES)
    lower_ends = (ends_five, *[sibling_of(piece, ends) for piece in pieces])
    sent_ends = {}
    moving_six = {}

    def from_ends(slot, after=()):
        sent_ends[slot] = partial(1, slot, upper_six, lower_ends, tilted, "ends", after)
        moving_six[goals[slot]] = start(sent_ends, goals[slot])

    for slot in slots:
        from_ends(slot, moving_five[goals[-1]] if slot == 1 else [])
    last = [moving_five[g] for g in goals[1:]]
    cuts = [4, 4]
    eigen_five, pieces = solve_five(own_five, last, "rest", [ends_five], cuts, [raised_six])
    lower_six = (eigen_five, *[sibling_of(piece, every) for piece in pieces])
    lowered_six = along(eigen_five, 1)
    sent_six = {}

    def from_rest(slot):
        if slot not in sent_six:
            sent_six[slot] = partial(1, slot, upper_six, lower_six, tilted, "rest")

    from_rest(0)
    beside_six = [[hop(sent_six[0][0], *aside)]] if skips else []
    for step in steps_to(far)[1:]:
        from_rest(slot_of(step, far))
    moving_six[far] = go_on(1, sent_six, moving_six[far], far)
    for slot in slots:
        from_rest(slot)
    sums_six = sums(1, upper_six, lower_six, local_six, occupation_six)
    for g in goals[1:]:
        moving_six[g] = go_on(1, sent_six, moving_six[g], g, [], last_cuts)
    updated_five = call(
        turn_kernel, [whole], [], [eigenbasis, turned, eigen_five], (), "back_five"
    )[0]
    own_six = call(
        finish_kernel,
        [whole],
        [occupation_six, bath_coefficients],
        [tilted, *sums_six, raised_six, lowered_six],
        (),
        "finish_six",
    )[0]
    previous = []
    for number in range(len(last_cuts)):
        last = [*[moving_six[g] for g in goals[1:]], moving_six[far], *beside_six]
        previous = solve_six(own_six, last, number, previous)
    return (updated_five, previous[0])


def solution(mesh):
    by_block = P(("ma", "mb"))
    in_specs = (by_block,) * 3 + (P(),) * 5 + (by_block,) * 8
    return jax.shard_map(
        body, mesh=mesh, in_specs=in_specs, out_specs=(by_block, by_block), check_vma=False
    )
```

```python
import functools
import math

import jax
import jax.numpy as jnp
from jax import lax
from jax.experimental import pallas as pl
from jax.experimental.pallas import tpu as pltpu
from jax.sharding import PartitionSpec as P

SMEM = pltpu.SMEM
VMEM = pltpu.VMEM
HALVES = 2
TOGETHER = 4


def split(x):
    high = x.astype(jnp.bfloat16)
    return high, (x - high.astype(jnp.float32)).astype(jnp.bfloat16)


def as_left(w):
    high, low = split(w)
    return jnp.concatenate([high, high, low], axis=1)


def as_right(w):
    high, low = split(w)
    return jnp.concatenate([high, high, low], axis=0)


def left_dot(w_left, x):
    high, low = split(x)
    return jnp.dot(
        w_left, jnp.concatenate([high, low, high], axis=0), preferred_element_type=jnp.float32
    )


def right_dot(x, w_right):
    high, low = split(x)
    return jnp.dot(
        jnp.concatenate([high, low, high], axis=1), w_right, preferred_element_type=jnp.float32
    )


def sandwich(w_left, real, imag, w_right):
    n = real.shape[0]
    right = right_dot(jnp.concatenate([real, imag], axis=0), w_right)
    both = left_dot(w_left, jnp.concatenate([right[:n], right[n:]], axis=1))
    return both[:, :n], both[:, n:]


def drive_of(mixed, turned, c_left, c_right):
    n = mixed.shape[-1]
    ahead = left_dot(
        c_left, jnp.concatenate([mixed[1] + turned[0], mixed[0] - turned[1]], axis=1)
    )
    behind = right_dot(
        jnp.concatenate([mixed[1] - turned[0], mixed[0] + turned[1]], axis=0), c_right
    )
    return behind[:n] - ahead[:, :n], ahead[:, n:] - behind[n:]


def add_requests(row, column, place, table, bath, upper, lower, mixed, turned):
    chip = place[0]
    core = place[1]
    for j in range(4):
        peer = table[row, column + j]
        spot = table[row, column + 4 + j]
        here = peer >> 1 == chip
        own, *pieces = upper if j < 2 else lower
        first = 0
        for number, source in enumerate([own, *pieces]):
            if number == 0:
                held = jnp.logical_and(here, peer & 1 == core)
                at = spot
            else:
                held = jnp.logical_and(here, peer & 1 != core)
                if len(pieces) > 1:
                    inside = jnp.logical_and(spot >= first, spot < first + source.shape[0])
                    held = jnp.logical_and(held, inside)
                at = spot - first
                first += source.shape[0]

            @pl.when(held)
            def _(j=j, source=source, at=at):
                if j < 2:
                    mixed[...] += source[at]
                else:
                    mode = j - 1
                    count = table[row, column + 6 + j].astype(jnp.float32)
                    mixed[...] += (count * bath[0, mode]) * source[at]
                    turned[...] += (count * bath[1, mode]) * source[at]


def partial_kernel(slot, column, role, counts, place, table, bath, *refs):
    upper, lower = refs[: counts[0]], refs[counts[0] : sum(counts)]
    c_ref, out, mixed, turned = refs[sum(counts) :]
    rows = upper[0].shape[0]
    together = mixed.shape[0]

    def work():
        c_left = as_left(c_ref[...])
        c_right = as_right(c_ref[...])

        @pl.loop(0, out.shape[0], step=together)
        def _(m):
            mixed[...] = jnp.zeros_like(mixed)
            turned[...] = jnp.zeros_like(turned)
            for u in range(together):
                add_requests(
                    place[3 + slot] * rows + m + u,
                    column,
                    place,
                    table,
                    bath,
                    upper,
                    lower,
                    mixed.at[u],
                    turned.at[u],
                )
            for u in range(together):
                real, imag = drive_of(mixed[u], turned[u], c_left, c_right)
                out[m + u, 0] = real
                out[m + u, 1] = imag

    by_role(role, place, work)


def by_role(role, place, work):
    if role == "all":
        work()
    elif role == "ends":
        pl.when(place[2] == 0)(work)
    else:
        pl.when(place[2] != 0)(work)


def sums_kernel(slot, column, counts, place, table, bath, nearby, occupation, *refs):
    upper, lower = refs[: counts[0]], refs[counts[0] : sum(counts)]
    mixed_out, turned_out = refs[sum(counts) :]
    rows = upper[0].shape[0]
    modes = bath.shape[1]

    @pl.loop(0, rows)
    def _(m):
        mixed = mixed_out.at[m]
        turned = turned_out.at[m]
        mixed[...] = upper[0][nearby[m, 0]]
        turned[...] = jnp.zeros_like(turned)
        add_requests(
            place[3 + slot] * rows + m, column, place, table, bath, upper, lower, mixed, turned
        )
        for k in range(3, modes):
            if k > 3:
                mixed[...] += upper[0][nearby[m, k - 3]]
            held = occupation[m, k]

            @pl.when(held > 0)
            def _(k=k, held=held):
                source = lower[0][nearby[m, modes - 3 + k - 3]]
                mixed[...] += (held.astype(jnp.float32) * bath[0, k]) * source
                turned[...] += (held.astype(jnp.float32) * bath[1, k]) * source


def own_drive(m, occupation, bath, mixed, turned, raised, lowered, c_left, c_right):
    count = occupation[m, 0].astype(jnp.float32)
    below = lowered[m]
    return drive_of(
        mixed[m] + raised[m] + (count * bath[0, 0]) * below,
        turned[m] + (count * bath[1, 0]) * below,
        c_left,
        c_right,
    )


def finish_kernel(occupation, bath, c_ref, mixed, turned, raised, lowered, out):
    c_left = as_left(c_ref[...])
    c_right = as_right(c_ref[...])
    for m in range(out.shape[0]):
        real, imag = own_drive(
            m, occupation, bath, mixed, turned, raised, lowered, c_left, c_right
        )
        out[m, 0] = real
        out[m, 1] = imag


def solved(real, imag, damping, splitting):
    inverse = 1.0 / (damping * damping + splitting * splitting)
    factor_real = -damping * inverse
    factor_imag = splitting * inverse
    return real * factor_real - imag * factor_imag, real * factor_imag + imag * factor_real


def damping_of(occupation, decay, m):
    damping = occupation[m, 0].astype(jnp.float32) * decay[0]
    for k in range(1, decay.shape[0]):
        damping = damping + occupation[m, k].astype(jnp.float32) * decay[k]
    return damping


def solve_five_kernel(
    counts, role, place, occupation, decay, e_row, e_column, e_ref, et_ref, own, *rest
):
    arrivals = []
    for count in counts[1:]:
        arrivals.append(rows_of(rest[:count]))
        rest = rest[count:]
    previous, (out, *pieces) = rest[: counts[0]], rest[counts[0] :]
    spots = rows_of(pieces)

    def work():
        splitting = e_column[...] - e_row[...]
        in_left = as_left(et_ref[...])
        in_right = as_right(e_ref[...])
        for m in range(out.shape[0]):
            real = own[m, 0]
            imag = own[m, 1]
            for arrival in arrivals:
                piece, row = arrival[m]
                real = real + piece[row, 0]
                imag = imag + piece[row, 1]
            real, imag = sandwich(in_left, real, imag, in_right)
            damping = damping_of(occupation, decay, m)
            real, imag = solved(real, imag, damping, splitting)
            out[m, 0] = real
            out[m, 1] = imag
            piece, row = spots[m]
            piece[row, 0] = real
            piece[row, 1] = imag

    by_role(role, place, work)
    if role == "rest":

        @pl.when(place[2] == 0)
        def _():
            out[...] = previous[0][...]
            first = 0
            for piece in pieces:
                piece[...] = previous[0][first : first + piece.shape[0]]
                first += piece.shape[0]


def solve_six_kernel(
    first, part_count, occupation, decay, e_row, e_column, e_ref, et_ref, own, *rest
):
    parts, out = rest[:part_count], rest[-1]
    splitting = e_column[...] - e_row[...]
    out_left = as_left(e_ref[...])
    out_right = as_right(et_ref[...])
    for m in range(out.shape[0]):
        real = own[m, 0]
        imag = own[m, 1]
        for part in parts:
            real = real + part[m, 0]
            imag = imag + part[m, 1]
        damping = damping_of(occupation, decay, first + m)
        real, imag = solved(real, imag, damping, splitting)
        real, imag = sandwich(out_left, real, imag, out_right)
        out[m, 0] = real
        out[m, 1] = imag


def turn_kernel(left_ref, right_ref, x, *outs):
    w_left = as_left(left_ref[...])
    w_right = as_right(right_ref[...])
    spots = [rows_of(outs[:1]), rows_of(outs[1:])] if len(outs) > 1 else [rows_of(outs)]
    for m in range(x.shape[0]):
        real, imag = sandwich(w_left, x[m, 0], x[m, 1], w_right)
        for spot in spots:
            out, row = spot[m]
            out[row, 0] = real
            out[row, 1] = imag


def turn_one_kernel(left_ref, right_ref, x, out):
    out[...] = left_dot(as_left(left_ref[...]), right_dot(x[...], as_right(right_ref[...])))


def rows_of(pieces):
    return [(piece, row) for piece in pieces for row in range(piece.shape[0])]


def add_kernel(counts, *refs):
    ours, theirs, outs = refs[: counts[0]], refs[counts[0] : sum(counts)], refs[sum(counts) :]
    for (a, i), (b, j), (out, k) in zip(rows_of(ours), rows_of(theirs), rows_of(outs)):
        out[k] = a[i] + b[j]


class Queue:
    def __init__(self):
        self.latest = []

    def call(
        self, kernel, outs, scalars, arrays, scratch=(), name=None, in_specs=None, after=(), **options
    ):
        waits = [w for w in [*self.latest, *after] if not any(w is a for a in arrays)]
        plain = pl.BlockSpec(memory_space=VMEM)
        count = len(scalars) + len(arrays)

        def without_waits(*refs):
            kernel(*refs[:count], *refs[count + len(waits) :])

        got = pl.pallas_call(
            without_waits,
            out_shape=outs,
            in_specs=[pl.BlockSpec(memory_space=SMEM)] * len(scalars)
            + (in_specs or [plain] * len(arrays))
            + [pl.BlockSpec(memory_space=pl.ANY)] * len(waits),
            out_specs=options.pop("out_specs", [plain] * len(outs)),
            scratch_shapes=scratch,
            compiler_params=pltpu.CompilerParams(vmem_limit_bytes=12 * 1024 * 1024),
            cost_estimate=pl.CostEstimate(flops=1, bytes_accessed=1, transcendentals=0),
            name=name,
            **options,
        )(*scalars, *arrays, *waits)
        self.latest = [got[0]]
        return got


def body(
    tier_four,
    tier_six,
    tier_seven,
    coupling,
    eigenbasis,
    energies,
    decay_rates,
    bath_coefficients,
    occupation_five,
    local_five,
    peers_five,
    places_five,
    occupation_six,
    local_six,
    peers_six,
    places_six,
):
    queue = Queue()
    call = queue.call
    rows = tier_four.shape[0]
    n = tier_four.shape[-1]
    peer_count = lax.axis_size("mb")
    row_count = lax.axis_size("ma")
    chips = peer_count // 2
    per = rows // HALVES
    whole = jax.ShapeDtypeStruct(tier_four.shape, jnp.float32)
    together = math.gcd(rows, TOGETHER)
    work_space = [pltpu.VMEM((together,) + tier_four.shape[1:], jnp.float32)] * 2

    def sibling_of(array, of_chips):
        return lax.ppermute(
            array, "mb", [(2 * i + c, 2 * i + 1 - c) for i in of_chips for c in range(2)]
        )

    def along(array, by):
        return lax.ppermute(array, "ma", [(i, (i + by) % row_count) for i in range(row_count)])

    def turn_line(array, by):
        return lax.ppermute(
            array, "mb", [(i, (i + 2 * by) % peer_count) for i in range(peer_count)]
        )

    def hop(array, *moves):
        pairs = []
        for start, stop in moves:
            for c in range(2):
                pairs.append((start * 2 + c, stop * 2 + c))
                pairs.append(((chips - 1 - start) * 2 + c, (chips - 1 - stop) * 2 + c))
        return lax.ppermute(array, "mb", pairs)

    mine = jnp.concatenate(
        [
            peers_five,
            places_five,
            occupation_five[:, 1:3],
            peers_six,
            places_six,
            occupation_six[:, 1:3],
        ],
        axis=1,
    )
    tables = [mine] + [turn_line(mine, by) for by in range(1, chips)]
    table = jnp.concatenate(tables, axis=0)
    columns = (0, mine.shape[1] // 2)

    goals = list(range(chips - 1, 0, -1))
    skips = chips > 3

    def slot_of(step, g):
        depth = min(step, chips - 1 - step)
        behind = step >= chips // 2
        return chips - 1 - g if behind else depth + chips - 1 - g

    index = lax.axis_index("mb")
    chip = index // 2
    mirrored = chip >= chips // 2
    depth = jnp.where(mirrored, chips - 1 - chip, chip)
    order = jnp.arange(chips, dtype=jnp.int32)
    seen = jnp.where(order < depth, order, chips - 1 - order + depth)
    goal = jnp.where(mirrored, chips - 1 - seen, seen)
    place = jnp.concatenate(
        [jnp.stack([chip, index % 2, depth]), (chip - goal + chips) % chips]
    ).astype(jnp.int32)

    def partial(tier, slot, upper, lower, c, role, after=()):
        return call(
            functools.partial(
                partial_kernel, slot, columns[tier], role, (len(upper), len(lower))
            ),
            [whole],
            [place, table, bath_coefficients],
            [*upper, *lower, c],
            work_space,
            f"partial_{tier}_{slot}_{role}",
            after=after,
        )

    def steps_to(g):
        last = g - 1 if skips and g == chips - 1 else g
        return list(range(last))

    def next_stop(step, g):
        return g if step == steps_to(g)[-1] else step + 1

    def start(sent, g):
        return [hop(array, (0, next_stop(0, g))) for array in sent[slot_of(0, g)]]

    def go_on(tier, sent, arrived, g, after=(), cuts=None):
        for step in steps_to(g)[1:]:
            parts = cuts if cuts and step == steps_to(g)[-1] else [rows]
            ours = sent[slot_of(step, g)]
            messages = call(
                functools.partial(add_kernel, (len(ours), len(arrived))),
                [jax.ShapeDtypeStruct((cut,) + whole.shape[1:], jnp.float32) for cut in parts],
                [],
                [*ours, *arrived],
                (),
                f"add_{tier}_{step}_{g}",
                after=after,
            )
            arrived = [hop(message, (step, next_stop(step, g))) for message in messages]
        return arrived

    def sums(tier, upper, lower, nearby, occupation):
        return call(
            functools.partial(sums_kernel, chips - 1, columns[tier], (len(upper), len(lower))),
            [whole, whole],
            [place, table, bath_coefficients, nearby.reshape(rows, -1), occupation],
            [*upper, *lower],
            (),
            f"sums_{tier}",
        )

    turned = jnp.transpose(eigenbasis)
    bases = [energies[None, :], energies[:, None], eigenbasis, turned]
    every = range(chips)
    ends = [0, chips - 1]

    def solve_five(own, last, role, previous, cuts, after=()):
        got = call(
            functools.partial(
                solve_five_kernel, [len(previous), *[len(pieces) for pieces in last]], role
            ),
            [whole]
            + [jax.ShapeDtypeStruct((cut,) + whole.shape[1:], jnp.float32) for cut in cuts],
            [place, occupation_five, decay_rates],
            [*bases, own, *[piece for pieces in last for piece in pieces], *previous],
            (),
            f"solve_five_{role}",
            after=after,
        )
        return got[0], got[1:]

    last_cuts = [per] * HALVES

    def solve_six(own, last, number, previous):
        cut = last_cuts[number]
        plain = pl.BlockSpec(memory_space=VMEM)
        first = sum(last_cuts[:number])
        block = pl.BlockSpec((cut,) + whole.shape[1:], lambda i: (first // cut, 0, 0, 0))
        parts = [pieces[number % len(pieces)] for pieces in last]
        arrays = [*bases, own, *parts, *previous]
        return call(
            functools.partial(solve_six_kernel, first, len(parts)),
            [whole],
            [occupation_six, decay_rates],
            arrays,
            (),
            f"solve_six_{number}",
            [plain] * len(bases)
            + [block]
            + [block if len(pieces) == 1 else plain for pieces in last]
            + [pl.BlockSpec(memory_space=pl.ANY)] * len(previous),
            out_specs=[block],
            grid=(1,),
            input_output_aliases={2 + len(arrays) - 1: 0} if previous else {},
        )

    raised_five = along(tier_six, -1)
    lowered_five = along(tier_four, 1)
    upper_five = (tier_six, sibling_of(tier_six, every))
    lower_five = (tier_four, sibling_of(tier_four, every))
    slots = range(chips - 1)
    far = goals[0]
    aside = [(far - 1, far)] if skips else []
    sent_five = {}
    moving_five = {}
    sent_five[0] = partial(0, 0, upper_five, lower_five, coupling, "all")
    moving_five[far] = [hop(array, (0, next_stop(0, far)), *aside) for array in sent_five[0]]
    beside_five = [moving_five[far]] if skips else []
    for slot in slots[1:]:
        sent_five[slot] = partial(0, slot, upper_five, lower_five, coupling, "all")
        moving_five[goals[slot]] = start(sent_five, goals[slot])
    sums_five = sums(0, upper_five, lower_five, local_five, occupation_five)
    tilted = call(
        turn_one_kernel,
        [jax.ShapeDtypeStruct((n, n), jnp.float32)],
        [],
        [turned, eigenbasis, coupling],
        (),
        "tilt_coupling",
    )[0]
    moving_five[far] = go_on(0, sent_five, moving_five[far], far)
    eigen_seven, *pieces = call(
        turn_kernel,
        [whole] + [jax.ShapeDtypeStruct((per,) + whole.shape[1:], jnp.float32)] * HALVES,
        [],
        [turned, eigenbasis, tier_seven],
        (),
        "tilt_seven",
        after=[raised_five],
    )
    pieces = [sibling_of(piece, every) for piece in pieces]
    upper_six = (eigen_seven, *pieces)
    raised_six = along(eigen_seven, -1)
    for g in goals[1:]:
        after = [lowered_five] if g == goals[-2] else []
        moving_five[g] = go_on(0, sent_five, moving_five[g], g, after)
    own_five = call(
        finish_kernel,
        [whole],
        [occupation_five, bath_coefficients],
        [coupling, *sums_five, raised_five, lowered_five],
        (),
        "finish_five",
        after=pieces,
    )[0]
    last = [moving_five[far], *beside_five]
    ends_five, pieces = solve_five(own_five, last, "ends", [], [per] * HALVES)
    lower_ends = (ends_five, *[sibling_of(piece, ends) for piece in pieces])
    sent_ends = {}
    moving_six = {}

    def from_ends(slot, after=()):
        sent_ends[slot] = partial(1, slot, upper_six, lower_ends, tilted, "ends", after)
        moving_six[goals[slot]] = start(sent_ends, goals[slot])

    for slot in slots:
        from_ends(slot, moving_five[goals[-1]] if slot == 1 else [])
    last = [moving_five[g] for g in goals[1:]]
    halves = [per] * HALVES
    eigen_five, pieces = solve_five(own_five, last, "rest", [ends_five], halves, [raised_six])
    lower_six = (eigen_five, *[sibling_of(piece, every) for piece in pieces])
    lowered_six = along(eigen_five, 1)
    sent_six = {}

    def from_rest(slot):
        if slot not in sent_six:
            sent_six[slot] = partial(1, slot, upper_six, lower_six, tilted, "rest")

    from_rest(0)
    beside_six = [[hop(sent_six[0][0], *aside)]] if skips else []
    for step in steps_to(far)[1:]:
        from_rest(slot_of(step, far))
    moving_six[far] = go_on(1, sent_six, moving_six[far], far)
    for slot in slots:
        from_rest(slot)
    sums_six = sums(1, upper_six, lower_six, local_six, occupation_six)
    for g in goals[1:]:
        moving_six[g] = go_on(1, sent_six, moving_six[g], g, [], last_cuts)
    updated_five = call(
        turn_kernel, [whole], [], [eigenbasis, turned, eigen_five], (), "back_five"
    )[0]
    own_six = call(
        finish_kernel,
        [whole],
        [occupation_six, bath_coefficients],
        [tilted, *sums_six, raised_six, lowered_six],
        (),
        "finish_six",
    )[0]
    previous = []
    for number in range(len(last_cuts)):
        last = [*[moving_six[g] for g in goals[1:]], moving_six[far], *beside_six]
        previous = solve_six(own_six, last, number, previous)
    return (updated_five, previous[0])


def solution(mesh):
    by_block = P(("ma", "mb"))
    in_specs = (by_block,) * 3 + (P(),) * 5 + (by_block,) * 8
    return jax.shard_map(
        body, mesh=mesh, in_specs=in_specs, out_specs=(by_block, by_block), check_vma=False
    )
```

```python
import functools
import math

import jax
import jax.numpy as jnp
from jax import lax
from jax.experimental import pallas as pl
from jax.experimental.pallas import tpu as pltpu
from jax.sharding import PartitionSpec as P

SMEM = pltpu.SMEM
VMEM = pltpu.VMEM
HALVES = 2
TOGETHER = 4


def split(x):
    high = x.astype(jnp.bfloat16)
    return high, (x - high.astype(jnp.float32)).astype(jnp.bfloat16)


def as_left(w):
    high, low = split(w)
    return jnp.concatenate([high, high, low], axis=1)


def as_right(w):
    high, low = split(w)
    return jnp.concatenate([high, high, low], axis=0)


def left_dot(w_left, x):
    high, low = split(x)
    return jnp.dot(
        w_left, jnp.concatenate([high, low, high], axis=0), preferred_element_type=jnp.float32
    )


def right_dot(x, w_right):
    high, low = split(x)
    return jnp.dot(
        jnp.concatenate([high, low, high], axis=1), w_right, preferred_element_type=jnp.float32
    )


def sandwich(w_left, real, imag, w_right):
    n = real.shape[0]
    right = right_dot(jnp.concatenate([real, imag], axis=0), w_right)
    both = left_dot(w_left, jnp.concatenate([right[:n], right[n:]], axis=1))
    return both[:, :n], both[:, n:]


def drive_of(mixed, turned, c_left, c_right):
    n = mixed.shape[-1]
    ahead = left_dot(
        c_left, jnp.concatenate([mixed[1] + turned[0], mixed[0] - turned[1]], axis=1)
    )
    behind = right_dot(
        jnp.concatenate([mixed[1] - turned[0], mixed[0] + turned[1]], axis=0), c_right
    )
    return behind[:n] - ahead[:, :n], ahead[:, n:] - behind[n:]


def add_requests(row, column, place, table, bath, upper, lower, mixed, turned):
    chip = place[0]
    core = place[1]
    for j in range(4):
        peer = table[row, column + j]
        spot = table[row, column + 4 + j]
        here = peer >> 1 == chip
        own, *pieces = upper if j < 2 else lower
        first = 0
        for number, source in enumerate([own, *pieces]):
            if number == 0:
                held = jnp.logical_and(here, peer & 1 == core)
                at = spot
            else:
                held = jnp.logical_and(here, peer & 1 != core)
                if len(pieces) > 1:
                    inside = jnp.logical_and(spot >= first, spot < first + source.shape[0])
                    held = jnp.logical_and(held, inside)
                at = spot - first
                first += source.shape[0]

            @pl.when(held)
            def _(j=j, source=source, at=at):
                if j < 2:
                    mixed[...] += source[at]
                else:
                    mode = j - 1
                    count = table[row, column + 6 + j].astype(jnp.float32)
                    mixed[...] += (count * bath[0, mode]) * source[at]
                    turned[...] += (count * bath[1, mode]) * source[at]


def partial_kernel(slot, column, role, counts, place, table, bath, *refs):
    upper, lower = refs[: counts[0]], refs[counts[0] : sum(counts)]
    c_ref, out, mixed, turned = refs[sum(counts) :]
    rows = upper[0].shape[0]
    together = mixed.shape[0]

    def work():
        c_left = as_left(c_ref[...])
        c_right = as_right(c_ref[...])

        @pl.loop(0, out.shape[0], step=together)
        def _(m):
            mixed[...] = jnp.zeros_like(mixed)
            turned[...] = jnp.zeros_like(turned)
            for u in range(together):
                add_requests(
                    place[3 + slot] * rows + m + u,
                    column,
                    place,
                    table,
                    bath,
                    upper,
                    lower,
                    mixed.at[u],
                    turned.at[u],
                )
            for u in range(together):
                real, imag = drive_of(mixed[u], turned[u], c_left, c_right)
                out[m + u, 0] = real
                out[m + u, 1] = imag

    by_role(role, place, work)


def by_role(role, place, work):
    if role == "all":
        work()
    elif role == "ends":
        pl.when(place[2] == 0)(work)
    else:
        pl.when(place[2] != 0)(work)


def sums_kernel(slot, column, counts, place, table, bath, nearby, occupation, *refs):
    upper, lower = refs[: counts[0]], refs[counts[0] : sum(counts)]
    mixed_out, turned_out = refs[sum(counts) :]
    rows = upper[0].shape[0]
    modes = bath.shape[1]

    @pl.loop(0, rows)
    def _(m):
        mixed = mixed_out.at[m]
        turned = turned_out.at[m]
        mixed[...] = upper[0][nearby[m, 0]]
        turned[...] = jnp.zeros_like(turned)
        add_requests(
            place[3 + slot] * rows + m, column, place, table, bath, upper, lower, mixed, turned
        )
        for k in range(3, modes):
            if k > 3:
                mixed[...] += upper[0][nearby[m, k - 3]]
            held = occupation[m, k]

            @pl.when(held > 0)
            def _(k=k, held=held):
                source = lower[0][nearby[m, modes - 3 + k - 3]]
                mixed[...] += (held.astype(jnp.float32) * bath[0, k]) * source
                turned[...] += (held.astype(jnp.float32) * bath[1, k]) * source


def own_drive(m, occupation, bath, mixed, turned, raised, lowered, c_left, c_right):
    count = occupation[m, 0].astype(jnp.float32)
    below = lowered[m]
    return drive_of(
        mixed[m] + raised[m] + (count * bath[0, 0]) * below,
        turned[m] + (count * bath[1, 0]) * below,
        c_left,
        c_right,
    )


def finish_kernel(occupation, bath, c_ref, mixed, turned, raised, lowered, out):
    c_left = as_left(c_ref[...])
    c_right = as_right(c_ref[...])
    for m in range(out.shape[0]):
        real, imag = own_drive(
            m, occupation, bath, mixed, turned, raised, lowered, c_left, c_right
        )
        out[m, 0] = real
        out[m, 1] = imag


def solved(real, imag, damping, splitting):
    inverse = 1.0 / (damping * damping + splitting * splitting)
    factor_real = -damping * inverse
    factor_imag = splitting * inverse
    return real * factor_real - imag * factor_imag, real * factor_imag + imag * factor_real


def damping_of(occupation, decay, m):
    damping = occupation[m, 0].astype(jnp.float32) * decay[0]
    for k in range(1, decay.shape[0]):
        damping = damping + occupation[m, k].astype(jnp.float32) * decay[k]
    return damping


def solve_five_kernel(
    counts, role, place, occupation, decay, e_row, e_column, e_ref, et_ref, own, *rest
):
    arrivals = []
    for count in counts[1:]:
        arrivals.append(rows_of(rest[:count]))
        rest = rest[count:]
    previous, (out, *pieces) = rest[: counts[0]], rest[counts[0] :]
    spots = rows_of(pieces)

    def work():
        splitting = e_column[...] - e_row[...]
        in_left = as_left(et_ref[...])
        in_right = as_right(e_ref[...])
        for m in range(out.shape[0]):
            real = own[m, 0]
            imag = own[m, 1]
            for arrival in arrivals:
                piece, row = arrival[m]
                real = real + piece[row, 0]
                imag = imag + piece[row, 1]
            real, imag = sandwich(in_left, real, imag, in_right)
            damping = damping_of(occupation, decay, m)
            real, imag = solved(real, imag, damping, splitting)
            out[m, 0] = real
            out[m, 1] = imag
            piece, row = spots[m]
            piece[row, 0] = real
            piece[row, 1] = imag

    by_role(role, place, work)
    if role == "rest":

        @pl.when(place[2] == 0)
        def _():
            out[...] = previous[0][...]
            first = 0
            for piece in pieces:
                piece[...] = previous[0][first : first + piece.shape[0]]
                first += piece.shape[0]


def solve_six_kernel(
    first, part_count, occupation, decay, e_row, e_column, e_ref, et_ref, own, *rest
):
    parts, out = rest[:part_count], rest[-1]
    splitting = e_column[...] - e_row[...]
    out_left = as_left(e_ref[...])
    out_right = as_right(et_ref[...])
    for m in range(out.shape[0]):
        real = own[m, 0]
        imag = own[m, 1]
        for part in parts:
            real = real + part[m, 0]
            imag = imag + part[m, 1]
        damping = damping_of(occupation, decay, first + m)
        real, imag = solved(real, imag, damping, splitting)
        real, imag = sandwich(out_left, real, imag, out_right)
        out[m, 0] = real
        out[m, 1] = imag


def turn_kernel(left_ref, right_ref, x, *outs):
    w_left = as_left(left_ref[...])
    w_right = as_right(right_ref[...])
    spots = [rows_of(outs[:1]), rows_of(outs[1:])] if len(outs) > 1 else [rows_of(outs)]
    for m in range(x.shape[0]):
        real, imag = sandwich(w_left, x[m, 0], x[m, 1], w_right)
        for spot in spots:
            out, row = spot[m]
            out[row, 0] = real
            out[row, 1] = imag


def turn_one_kernel(left_ref, right_ref, x, out):
    out[...] = left_dot(as_left(left_ref[...]), right_dot(x[...], as_right(right_ref[...])))


def rows_of(pieces):
    return [(piece, row) for piece in pieces for row in range(piece.shape[0])]


def add_kernel(counts, *refs):
    ours, theirs, outs = refs[: counts[0]], refs[counts[0] : sum(counts)], refs[sum(counts) :]
    for (a, i), (b, j), (out, k) in zip(rows_of(ours), rows_of(theirs), rows_of(outs)):
        out[k] = a[i] + b[j]


class Queue:
    def __init__(self):
        self.latest = []

    def call(
        self, kernel, outs, scalars, arrays, scratch=(), name=None, in_specs=None, after=(), **options
    ):
        waits = [w for w in [*self.latest, *after] if not any(w is a for a in arrays)]
        plain = pl.BlockSpec(memory_space=VMEM)
        count = len(scalars) + len(arrays)

        def without_waits(*refs):
            kernel(*refs[:count], *refs[count + len(waits) :])

        got = pl.pallas_call(
            without_waits,
            out_shape=outs,
            in_specs=[pl.BlockSpec(memory_space=SMEM)] * len(scalars)
            + (in_specs or [plain] * len(arrays))
            + [pl.BlockSpec(memory_space=pl.ANY)] * len(waits),
            out_specs=options.pop("out_specs", [plain] * len(outs)),
            scratch_shapes=scratch,
            compiler_params=pltpu.CompilerParams(vmem_limit_bytes=12 * 1024 * 1024),
            cost_estimate=pl.CostEstimate(flops=1, bytes_accessed=1, transcendentals=0),
            name=name,
            **options,
        )(*scalars, *arrays, *waits)
        self.latest = [got[0]]
        return got


def body(
    tier_four,
    tier_six,
    tier_seven,
    coupling,
    eigenbasis,
    energies,
    decay_rates,
    bath_coefficients,
    occupation_five,
    local_five,
    peers_five,
    places_five,
    occupation_six,
    local_six,
    peers_six,
    places_six,
):
    queue = Queue()
    call = queue.call
    rows = tier_four.shape[0]
    n = tier_four.shape[-1]
    peer_count = lax.axis_size("mb")
    row_count = lax.axis_size("ma")
    chips = peer_count // 2
    per = rows // HALVES
    whole = jax.ShapeDtypeStruct(tier_four.shape, jnp.float32)
    together = math.gcd(rows, TOGETHER)
    work_space = [pltpu.VMEM((together,) + tier_four.shape[1:], jnp.float32)] * 2

    def sibling_of(array, of_chips):
        return lax.ppermute(
            array, "mb", [(2 * i + c, 2 * i + 1 - c) for i in of_chips for c in range(2)]
        )

    def along(array, by):
        return lax.ppermute(array, "ma", [(i, (i + by) % row_count) for i in range(row_count)])

    def turn_line(array, by):
        return lax.ppermute(
            array, "mb", [(i, (i + 2 * by) % peer_count) for i in range(peer_count)]
        )

    def hop(array, *moves):
        pairs = []
        for start, stop in moves:
            for c in range(2):
                pairs.append((start * 2 + c, stop * 2 + c))
                pairs.append(((chips - 1 - start) * 2 + c, (chips - 1 - stop) * 2 + c))
        return lax.ppermute(array, "mb", pairs)

    mine = jnp.concatenate(
        [
            peers_five,
            places_five,
            occupation_five[:, 1:3],
            peers_six,
            places_six,
            occupation_six[:, 1:3],
        ],
        axis=1,
    )
    tables = [mine] + [turn_line(mine, by) for by in range(1, chips)]
    table = jnp.concatenate(tables, axis=0)
    columns = (0, mine.shape[1] // 2)

    goals = list(range(chips - 1, 0, -1))
    skips = chips > 3

    def slot_of(step, g):
        depth = min(step, chips - 1 - step)
        behind = step >= chips // 2
        return chips - 1 - g if behind else depth + chips - 1 - g

    index = lax.axis_index("mb")
    chip = index // 2
    mirrored = chip >= chips // 2
    depth = jnp.where(mirrored, chips - 1 - chip, chip)
    order = jnp.arange(chips, dtype=jnp.int32)
    seen = jnp.where(order < depth, order, chips - 1 - order + depth)
    goal = jnp.where(mirrored, chips - 1 - seen, seen)
    place = jnp.concatenate(
        [jnp.stack([chip, index % 2, depth]), (chip - goal + chips) % chips]
    ).astype(jnp.int32)

    def partial(tier, slot, upper, lower, c, role, after=()):
        return call(
            functools.partial(
                partial_kernel, slot, columns[tier], role, (len(upper), len(lower))
            ),
            [whole],
            [place, table, bath_coefficients],
            [*upper, *lower, c],
            work_space,
            f"partial_{tier}_{slot}_{role}",
            after=after,
        )

    def steps_to(g):
        last = g - 1 if skips and g == chips - 1 else g
        return list(range(last))

    def next_stop(step, g):
        return g if step == steps_to(g)[-1] else step + 1

    def start(sent, g):
        return [hop(array, (0, next_stop(0, g))) for array in sent[slot_of(0, g)]]

    def go_on(tier, sent, arrived, g, after=(), cuts=None):
        for step in steps_to(g)[1:]:
            parts = cuts if cuts and step == steps_to(g)[-1] else [rows]
            ours = sent[slot_of(step, g)]
            messages = call(
                functools.partial(add_kernel, (len(ours), len(arrived))),
                [jax.ShapeDtypeStruct((cut,) + whole.shape[1:], jnp.float32) for cut in parts],
                [],
                [*ours, *arrived],
                (),
                f"add_{tier}_{step}_{g}",
                after=after,
            )
            arrived = [hop(message, (step, next_stop(step, g))) for message in messages]
        return arrived

    def sums(tier, upper, lower, nearby, occupation):
        return call(
            functools.partial(sums_kernel, chips - 1, columns[tier], (len(upper), len(lower))),
            [whole, whole],
            [place, table, bath_coefficients, nearby.reshape(rows, -1), occupation],
            [*upper, *lower],
            (),
            f"sums_{tier}",
        )

    turned = jnp.transpose(eigenbasis)
    bases = [energies[None, :], energies[:, None], eigenbasis, turned]
    every = range(chips)
    ends = [0, chips - 1]

    def solve_five(own, last, role, previous, cuts, after=()):
        got = call(
            functools.partial(
                solve_five_kernel, [len(previous), *[len(pieces) for pieces in last]], role
            ),
            [whole]
            + [jax.ShapeDtypeStruct((cut,) + whole.shape[1:], jnp.float32) for cut in cuts],
            [place, occupation_five, decay_rates],
            [*bases, own, *[piece for pieces in last for piece in pieces], *previous],
            (),
            f"solve_five_{role}",
            after=after,
        )
        return got[0], got[1:]

    last_cuts = [per] * HALVES

    def solve_six(own, last, number, previous):
        cut = last_cuts[number]
        plain = pl.BlockSpec(memory_space=VMEM)
        first = sum(last_cuts[:number])
        block = pl.BlockSpec((cut,) + whole.shape[1:], lambda i: (first // cut, 0, 0, 0))
        parts = [pieces[number % len(pieces)] for pieces in last]
        arrays = [*bases, own, *parts, *previous]
        return call(
            functools.partial(solve_six_kernel, first, len(parts)),
            [whole],
            [occupation_six, decay_rates],
            arrays,
            (),
            f"solve_six_{number}",
            [plain] * len(bases)
            + [block]
            + [block if len(pieces) == 1 else plain for pieces in last]
            + [pl.BlockSpec(memory_space=pl.ANY)] * len(previous),
            out_specs=[block],
            grid=(1,),
            input_output_aliases={2 + len(arrays) - 1: 0} if previous else {},
        )

    raised_five = along(tier_six, -1)
    lowered_five = along(tier_four, 1)
    upper_five = (tier_six, sibling_of(tier_six, every))
    lower_five = (tier_four, sibling_of(tier_four, every))
    slots = range(chips - 1)
    far = goals[0]
    aside = [(far - 1, far)] if skips else []
    sent_five = {}
    moving_five = {}
    sent_five[0] = partial(0, 0, upper_five, lower_five, coupling, "all")
    moving_five[far] = [hop(array, (0, next_stop(0, far)), *aside) for array in sent_five[0]]
    beside_five = [moving_five[far]] if skips else []
    for slot in slots[1:]:
        sent_five[slot] = partial(0, slot, upper_five, lower_five, coupling, "all")
        moving_five[goals[slot]] = start(sent_five, goals[slot])
    sums_five = sums(0, upper_five, lower_five, local_five, occupation_five)
    moving_five[far] = go_on(0, sent_five, moving_five[far], far)
    eigen_seven, *pieces = call(
        turn_kernel,
        [whole] + [jax.ShapeDtypeStruct((per,) + whole.shape[1:], jnp.float32)] * HALVES,
        [],
        [turned, eigenbasis, tier_seven],
        (),
        "tilt_seven",
        after=[raised_five],
    )
    pieces = [sibling_of(piece, every) for piece in pieces]
    upper_six = (eigen_seven, *pieces)
    raised_six = along(eigen_seven, -1)
    tilted = call(
        turn_one_kernel,
        [jax.ShapeDtypeStruct((n, n), jnp.float32)],
        [],
        [turned, eigenbasis, coupling],
        (),
        "tilt_coupling",
        after=pieces,
    )[0]
    for g in goals[1:]:
        moving_five[g] = go_on(0, sent_five, moving_five[g], g)
    own_five = call(
        finish_kernel,
        [whole],
        [occupation_five, bath_coefficients],
        [coupling, *sums_five, raised_five, lowered_five],
        (),
        "finish_five",
    )[0]
    last = [moving_five[far], *beside_five]
    ends_five, pieces = solve_five(own_five, last, "ends", [], [per] * HALVES)
    lower_ends = (ends_five, *[sibling_of(piece, ends) for piece in pieces])
    sent_ends = {}
    moving_six = {}

    def from_ends(slot, after=()):
        sent_ends[slot] = partial(1, slot, upper_six, lower_ends, tilted, "ends", after)
        moving_six[goals[slot]] = start(sent_ends, goals[slot])

    for slot in slots:
        from_ends(slot, moving_five[goals[-1]] if slot == 1 else [])
    last = [moving_five[g] for g in goals[1:]]
    halves = [per] * HALVES
    eigen_five, pieces = solve_five(own_five, last, "rest", [ends_five], halves, [raised_six])
    lower_six = (eigen_five, *[sibling_of(piece, every) for piece in pieces])
    lowered_six = along(eigen_five, 1)
    sent_six = {}

    def from_rest(slot):
        if slot not in sent_six:
            sent_six[slot] = partial(1, slot, upper_six, lower_six, tilted, "rest")

    from_rest(0)
    beside_six = [[hop(sent_six[0][0], *aside)]] if skips else []
    for step in steps_to(far)[1:]:
        from_rest(slot_of(step, far))
    moving_six[far] = go_on(1, sent_six, moving_six[far], far)
    for slot in slots:
        from_rest(slot)
    sums_six = sums(1, upper_six, lower_six, local_six, occupation_six)
    for g in goals[1:]:
        moving_six[g] = go_on(1, sent_six, moving_six[g], g, [], last_cuts)
    updated_five = call(
        turn_kernel, [whole], [], [eigenbasis, turned, eigen_five], (), "back_five"
    )[0]
    own_six = call(
        finish_kernel,
        [whole],
        [occupation_six, bath_coefficients],
        [tilted, *sums_six, raised_six, lowered_six],
        (),
        "finish_six",
    )[0]
    previous = []
    for number in range(len(last_cuts)):
        last = [*[moving_six[g] for g in goals[1:]], moving_six[far], *beside_six]
        previous = solve_six(own_six, last, number, previous)
    return (updated_five, previous[0])


def solution(mesh):
    by_block = P(("ma", "mb"))
    in_specs = (by_block,) * 3 + (P(),) * 5 + (by_block,) * 8
    return jax.shard_map(
        body, mesh=mesh, in_specs=in_specs, out_specs=(by_block, by_block), check_vma=False
    )
```

```python
import functools
import math

import jax
import jax.numpy as jnp
from jax import lax
from jax.experimental import pallas as pl
from jax.experimental.pallas import tpu as pltpu
from jax.sharding import PartitionSpec as P

SMEM = pltpu.SMEM
VMEM = pltpu.VMEM
HALVES = 2
TOGETHER = 4


def split(x):
    high = x.astype(jnp.bfloat16)
    return high, (x - high.astype(jnp.float32)).astype(jnp.bfloat16)


def as_left(w):
    high, low = split(w)
    return jnp.concatenate([high, high, low], axis=1)


def as_right(w):
    high, low = split(w)
    return jnp.concatenate([high, high, low], axis=0)


def left_dot(w_left, x):
    high, low = split(x)
    return jnp.dot(
        w_left, jnp.concatenate([high, low, high], axis=0), preferred_element_type=jnp.float32
    )


def right_dot(x, w_right):
    high, low = split(x)
    return jnp.dot(
        jnp.concatenate([high, low, high], axis=1), w_right, preferred_element_type=jnp.float32
    )


def sandwich(w_left, real, imag, w_right):
    n = real.shape[0]
    right = right_dot(jnp.concatenate([real, imag], axis=0), w_right)
    both = left_dot(w_left, jnp.concatenate([right[:n], right[n:]], axis=1))
    return both[:, :n], both[:, n:]


def drive_of(mixed, turned, c_left, c_right):
    n = mixed.shape[-1]
    ahead = left_dot(
        c_left, jnp.concatenate([mixed[1] + turned[0], mixed[0] - turned[1]], axis=1)
    )
    behind = right_dot(
        jnp.concatenate([mixed[1] - turned[0], mixed[0] + turned[1]], axis=0), c_right
    )
    return behind[:n] - ahead[:, :n], ahead[:, n:] - behind[n:]


def add_requests(row, column, place, table, bath, upper, lower, mixed, turned):
    chip = place[0]
    core = place[1]
    for j in range(4):
        peer = table[row, column + j]
        spot = table[row, column + 4 + j]
        here = peer >> 1 == chip
        own, *pieces = upper if j < 2 else lower
        first = 0
        for number, source in enumerate([own, *pieces]):
            if number == 0:
                held = jnp.logical_and(here, peer & 1 == core)
                at = spot
            else:
                held = jnp.logical_and(here, peer & 1 != core)
                if len(pieces) > 1:
                    inside = jnp.logical_and(spot >= first, spot < first + source.shape[0])
                    held = jnp.logical_and(held, inside)
                at = spot - first
                first += source.shape[0]

            @pl.when(held)
            def _(j=j, source=source, at=at):
                if j < 2:
                    mixed[...] += source[at]
                else:
                    mode = j - 1
                    count = table[row, column + 6 + j].astype(jnp.float32)
                    mixed[...] += (count * bath[0, mode]) * source[at]
                    turned[...] += (count * bath[1, mode]) * source[at]


def partial_kernel(slot, column, role, counts, place, table, bath, *refs):
    upper, lower = refs[: counts[0]], refs[counts[0] : sum(counts)]
    c_ref, out, mixed, turned = refs[sum(counts) :]
    rows = upper[0].shape[0]
    together = mixed.shape[0]

    def work():
        c_left = as_left(c_ref[...])
        c_right = as_right(c_ref[...])

        @pl.loop(0, out.shape[0], step=together)
        def _(m):
            mixed[...] = jnp.zeros_like(mixed)
            turned[...] = jnp.zeros_like(turned)
            for u in range(together):
                add_requests(
                    place[3 + slot] * rows + m + u,
                    column,
                    place,
                    table,
                    bath,
                    upper,
                    lower,
                    mixed.at[u],
                    turned.at[u],
                )
            for u in range(together):
                real, imag = drive_of(mixed[u], turned[u], c_left, c_right)
                out[m + u, 0] = real
                out[m + u, 1] = imag

    by_role(role, place, work)


def by_role(role, place, work):
    if role == "all":
        work()
    elif role == "ends":
        pl.when(place[2] == 0)(work)
    else:
        pl.when(place[2] != 0)(work)


def sums_kernel(slot, column, counts, place, table, bath, nearby, occupation, *refs):
    upper, lower = refs[: counts[0]], refs[counts[0] : sum(counts)]
    mixed_out, turned_out = refs[sum(counts) :]
    rows = upper[0].shape[0]
    modes = bath.shape[1]

    @pl.loop(0, rows)
    def _(m):
        mixed = mixed_out.at[m]
        turned = turned_out.at[m]
        mixed[...] = upper[0][nearby[m, 0]]
        turned[...] = jnp.zeros_like(turned)
        add_requests(
            place[3 + slot] * rows + m, column, place, table, bath, upper, lower, mixed, turned
        )
        for k in range(3, modes):
            if k > 3:
                mixed[...] += upper[0][nearby[m, k - 3]]
            held = occupation[m, k]

            @pl.when(held > 0)
            def _(k=k, held=held):
                source = lower[0][nearby[m, modes - 3 + k - 3]]
                mixed[...] += (held.astype(jnp.float32) * bath[0, k]) * source
                turned[...] += (held.astype(jnp.float32) * bath[1, k]) * source


def own_drive(m, occupation, bath, mixed, turned, raised, lowered, c_left, c_right):
    count = occupation[m, 0].astype(jnp.float32)
    below = lowered[m]
    return drive_of(
        mixed[m] + raised[m] + (count * bath[0, 0]) * below,
        turned[m] + (count * bath[1, 0]) * below,
        c_left,
        c_right,
    )


def finish_kernel(occupation, bath, c_ref, mixed, turned, raised, lowered, out):
    c_left = as_left(c_ref[...])
    c_right = as_right(c_ref[...])
    for m in range(out.shape[0]):
        real, imag = own_drive(
            m, occupation, bath, mixed, turned, raised, lowered, c_left, c_right
        )
        out[m, 0] = real
        out[m, 1] = imag


def solved(real, imag, damping, splitting):
    inverse = 1.0 / (damping * damping + splitting * splitting)
    factor_real = -damping * inverse
    factor_imag = splitting * inverse
    return real * factor_real - imag * factor_imag, real * factor_imag + imag * factor_real


def damping_of(occupation, decay, m):
    damping = occupation[m, 0].astype(jnp.float32) * decay[0]
    for k in range(1, decay.shape[0]):
        damping = damping + occupation[m, k].astype(jnp.float32) * decay[k]
    return damping


def solve_five_kernel(
    counts, role, place, occupation, decay, e_row, e_column, e_ref, et_ref, own, *rest
):
    arrivals = []
    for count in counts[1:]:
        arrivals.append(rows_of(rest[:count]))
        rest = rest[count:]
    previous, (out, *pieces) = rest[: counts[0]], rest[counts[0] :]
    spots = rows_of(pieces)

    def work():
        splitting = e_column[...] - e_row[...]
        in_left = as_left(et_ref[...])
        in_right = as_right(e_ref[...])
        for m in range(out.shape[0]):
            real = own[m, 0]
            imag = own[m, 1]
            for arrival in arrivals:
                piece, row = arrival[m]
                real = real + piece[row, 0]
                imag = imag + piece[row, 1]
            real, imag = sandwich(in_left, real, imag, in_right)
            damping = damping_of(occupation, decay, m)
            real, imag = solved(real, imag, damping, splitting)
            out[m, 0] = real
            out[m, 1] = imag
            piece, row = spots[m]
            piece[row, 0] = real
            piece[row, 1] = imag

    by_role(role, place, work)
    if role == "rest":

        @pl.when(place[2] == 0)
        def _():
            out[...] = previous[0][...]
            first = 0
            for piece in pieces:
                piece[...] = previous[0][first : first + piece.shape[0]]
                first += piece.shape[0]


def solve_six_kernel(
    first, part_count, occupation, decay, e_row, e_column, e_ref, et_ref, own, *rest
):
    parts, out = rest[:part_count], rest[-1]
    splitting = e_column[...] - e_row[...]
    out_left = as_left(e_ref[...])
    out_right = as_right(et_ref[...])
    for m in range(out.shape[0]):
        real = own[m, 0]
        imag = own[m, 1]
        for part in parts:
            real = real + part[m, 0]
            imag = imag + part[m, 1]
        damping = damping_of(occupation, decay, first + m)
        real, imag = solved(real, imag, damping, splitting)
        real, imag = sandwich(out_left, real, imag, out_right)
        out[m, 0] = real
        out[m, 1] = imag


def turn_kernel(left_ref, right_ref, x, *outs):
    w_left = as_left(left_ref[...])
    w_right = as_right(right_ref[...])
    spots = [rows_of(outs[:1]), rows_of(outs[1:])] if len(outs) > 1 else [rows_of(outs)]
    for m in range(x.shape[0]):
        real, imag = sandwich(w_left, x[m, 0], x[m, 1], w_right)
        for spot in spots:
            out, row = spot[m]
            out[row, 0] = real
            out[row, 1] = imag


def turn_one_kernel(left_ref, right_ref, x, out):
    out[...] = left_dot(as_left(left_ref[...]), right_dot(x[...], as_right(right_ref[...])))


def rows_of(pieces):
    return [(piece, row) for piece in pieces for row in range(piece.shape[0])]


def add_kernel(counts, *refs):
    ours, theirs, outs = refs[: counts[0]], refs[counts[0] : sum(counts)], refs[sum(counts) :]
    for (a, i), (b, j), (out, k) in zip(rows_of(ours), rows_of(theirs), rows_of(outs)):
        out[k] = a[i] + b[j]


class Queue:
    def __init__(self):
        self.latest = []

    def call(
        self, kernel, outs, scalars, arrays, scratch=(), name=None, in_specs=None, after=(), **options
    ):
        waits = [w for w in [*self.latest, *after] if not any(w is a for a in arrays)]
        plain = pl.BlockSpec(memory_space=VMEM)
        count = len(scalars) + len(arrays)

        def without_waits(*refs):
            rest = refs[count + len(waits) :]
            kernel(*refs[:count], *rest[: len(outs)], *rest[len(outs) + 1 :])
            rest[len(outs)][...] = jnp.zeros_like(rest[len(outs)])

        got = pl.pallas_call(
            without_waits,
            out_shape=[*outs, jax.ShapeDtypeStruct((8, 128), jnp.float32)],
            in_specs=[pl.BlockSpec(memory_space=SMEM)] * len(scalars)
            + (in_specs or [plain] * len(arrays))
            + [pl.BlockSpec(memory_space=pl.ANY)] * len(waits),
            out_specs=options.pop("out_specs", [plain] * len(outs)) + [plain],
            scratch_shapes=scratch,
            compiler_params=pltpu.CompilerParams(vmem_limit_bytes=12 * 1024 * 1024),
            cost_estimate=pl.CostEstimate(flops=1, bytes_accessed=1, transcendentals=0),
            name=name,
            **options,
        )(*scalars, *arrays, *waits)
        self.latest = [got[-1]]
        return got[:-1]


def body(
    tier_four,
    tier_six,
    tier_seven,
    coupling,
    eigenbasis,
    energies,
    decay_rates,
    bath_coefficients,
    occupation_five,
    local_five,
    peers_five,
    places_five,
    occupation_six,
    local_six,
    peers_six,
    places_six,
):
    queue = Queue()
    call = queue.call
    rows = tier_four.shape[0]
    n = tier_four.shape[-1]
    peer_count = lax.axis_size("mb")
    row_count = lax.axis_size("ma")
    chips = peer_count // 2
    per = rows // HALVES
    whole = jax.ShapeDtypeStruct(tier_four.shape, jnp.float32)
    together = math.gcd(rows, TOGETHER)
    work_space = [pltpu.VMEM((together,) + tier_four.shape[1:], jnp.float32)] * 2

    def sibling_of(array, of_chips):
        return lax.ppermute(
            array, "mb", [(2 * i + c, 2 * i + 1 - c) for i in of_chips for c in range(2)]
        )

    def along(array, by):
        return lax.ppermute(array, "ma", [(i, (i + by) % row_count) for i in range(row_count)])

    def turn_line(array, by):
        return lax.ppermute(
            array, "mb", [(i, (i + 2 * by) % peer_count) for i in range(peer_count)]
        )

    def hop(array, *moves):
        pairs = []
        for start, stop in moves:
            for c in range(2):
                pairs.append((start * 2 + c, stop * 2 + c))
                pairs.append(((chips - 1 - start) * 2 + c, (chips - 1 - stop) * 2 + c))
        return lax.ppermute(array, "mb", pairs)

    mine = jnp.concatenate(
        [
            peers_five,
            places_five,
            occupation_five[:, 1:3],
            peers_six,
            places_six,
            occupation_six[:, 1:3],
        ],
        axis=1,
    )
    tables = [mine] + [turn_line(mine, by) for by in range(chips - 1, 0, -1)]
    table = jnp.concatenate(tables, axis=0)
    columns = (0, mine.shape[1] // 2)

    goals = list(range(chips - 1, 0, -1))
    skips = chips > 3

    def slot_of(step, g):
        depth = min(step, chips - 1 - step)
        behind = step >= chips // 2
        return chips - 1 - g if behind else depth + chips - 1 - g

    index = lax.axis_index("mb")
    chip = index // 2
    mirrored = chip >= chips // 2
    depth = jnp.where(mirrored, chips - 1 - chip, chip)
    order = jnp.arange(chips, dtype=jnp.int32)
    seen = jnp.where(order < depth, order, chips - 1 - order + depth)
    goal = jnp.where(mirrored, chips - 1 - seen, seen)
    place = jnp.concatenate(
        [jnp.stack([chip, index % 2, depth]), (goal - chip + chips) % chips]
    ).astype(jnp.int32)

    def partial(tier, slot, upper, lower, c, role, after=()):
        return call(
            functools.partial(
                partial_kernel, slot, columns[tier], role, (len(upper), len(lower))
            ),
            [whole],
            [place, table, bath_coefficients],
            [*upper, *lower, c],
            work_space,
            f"partial_{tier}_{slot}_{role}",
            after=after,
        )

    def steps_to(g):
        last = g - 1 if skips and g == chips - 1 else g
        return list(range(last))

    def next_stop(step, g):
        return g if step == steps_to(g)[-1] else step + 1

    def start(sent, g):
        return [hop(array, (0, next_stop(0, g))) for array in sent[slot_of(0, g)]]

    def go_on(tier, sent, arrived, g, after=(), cuts=None):
        for step in steps_to(g)[1:]:
            parts = cuts if cuts and step == steps_to(g)[-1] else [rows]
            ours = sent[slot_of(step, g)]
            messages = call(
                functools.partial(add_kernel, (len(ours), len(arrived))),
                [jax.ShapeDtypeStruct((cut,) + whole.shape[1:], jnp.float32) for cut in parts],
                [],
                [*ours, *arrived],
                (),
                f"add_{tier}_{step}_{g}",
                after=after,
            )
            arrived = [hop(message, (step, next_stop(step, g))) for message in messages]
        return arrived

    def sums(tier, upper, lower, nearby, occupation):
        return call(
            functools.partial(sums_kernel, chips - 1, columns[tier], (len(upper), len(lower))),
            [whole, whole],
            [place, table, bath_coefficients, nearby.reshape(rows, -1), occupation],
            [*upper, *lower],
            (),
            f"sums_{tier}",
        )

    turned = jnp.transpose(eigenbasis)
    bases = [energies[None, :], energies[:, None], eigenbasis, turned]
    every = range(chips)
    ends = [0, chips - 1]

    def solve_five(own, last, role, previous, cuts, after=()):
        got = call(
            functools.partial(
                solve_five_kernel, [len(previous), *[len(pieces) for pieces in last]], role
            ),
            [whole]
            + [jax.ShapeDtypeStruct((cut,) + whole.shape[1:], jnp.float32) for cut in cuts],
            [place, occupation_five, decay_rates],
            [*bases, own, *[piece for pieces in last for piece in pieces], *previous],
            (),
            f"solve_five_{role}",
            after=after,
        )
        return got[0], got[1:]

    last_cuts = [rows - rows // 4, rows // 4]

    def solve_six(own, last, number, previous):
        cut = last_cuts[number]
        plain = pl.BlockSpec(memory_space=VMEM)
        first = sum(last_cuts[:number])
        block = pl.BlockSpec((cut,) + whole.shape[1:], lambda i: (first // cut, 0, 0, 0))
        parts = [pieces[number % len(pieces)] for pieces in last]
        arrays = [*bases, own, *parts, *previous]
        return call(
            functools.partial(solve_six_kernel, first, len(parts)),
            [whole],
            [occupation_six, decay_rates],
            arrays,
            (),
            f"solve_six_{number}",
            [plain] * len(bases)
            + [block]
            + [block if len(pieces) == 1 else plain for pieces in last]
            + [pl.BlockSpec(memory_space=pl.ANY)] * len(previous),
            out_specs=[block],
            grid=(1,),
            input_output_aliases={2 + len(arrays) - 1: 0} if previous else {},
        )

    raised_five = along(tier_six, -1)
    lowered_five = along(tier_four, 1)
    upper_five = (tier_six, sibling_of(tier_six, every))
    lower_five = (tier_four, sibling_of(tier_four, every))
    slots = range(chips - 1)
    far = goals[0]
    aside = [(far - 1, far)] if skips else []
    sent_five = {}
    moving_five = {}
    sent_five[0] = partial(0, 0, upper_five, lower_five, coupling, "all")
    moving_five[far] = [hop(array, (0, next_stop(0, far)), *aside) for array in sent_five[0]]
    beside_five = [moving_five[far]] if skips else []
    for slot in slots[1:]:
        sent_five[slot] = partial(0, slot, upper_five, lower_five, coupling, "all")
        moving_five[goals[slot]] = start(sent_five, goals[slot])
    sums_five = sums(0, upper_five, lower_five, local_five, occupation_five)
    moving_five[far] = go_on(0, sent_five, moving_five[far], far)
    eigen_seven, *pieces = call(
        turn_kernel,
        [whole] + [jax.ShapeDtypeStruct((per,) + whole.shape[1:], jnp.float32)] * HALVES,
        [],
        [turned, eigenbasis, tier_seven],
        (),
        "tilt_seven",
        after=[raised_five],
    )
    pieces = [sibling_of(piece, every) for piece in pieces]
    upper_six = (eigen_seven, *pieces)
    raised_six = along(eigen_seven, -1)
    tilted = call(
        turn_one_kernel,
        [jax.ShapeDtypeStruct((n, n), jnp.float32)],
        [],
        [turned, eigenbasis, coupling],
        (),
        "tilt_coupling",
        after=pieces,
    )[0]
    for g in goals[1:]:
        moving_five[g] = go_on(0, sent_five, moving_five[g], g)
    own_five = call(
        finish_kernel,
        [whole],
        [occupation_five, bath_coefficients],
        [coupling, *sums_five, raised_five, lowered_five],
        (),
        "finish_five",
    )[0]
    last = [moving_five[far], *beside_five]
    ends_five, pieces = solve_five(own_five, last, "ends", [], [per] * HALVES)
    lower_ends = (ends_five, *[sibling_of(piece, ends) for piece in pieces])
    sent_ends = {}
    moving_six = {}

    def from_ends(slot, after=()):
        sent_ends[slot] = partial(1, slot, upper_six, lower_ends, tilted, "ends", after)
        moving_six[goals[slot]] = start(sent_ends, goals[slot])

    for slot in slots:
        from_ends(slot, moving_five[goals[-1]] if slot == 1 else [])
    last = [moving_five[g] for g in goals[1:]]
    halves = [per] * HALVES
    eigen_five, pieces = solve_five(own_five, last, "rest", [ends_five], halves, [raised_six])
    lower_six = (eigen_five, *[sibling_of(piece, every) for piece in pieces])
    lowered_six = along(eigen_five, 1)
    sent_six = {}

    def from_rest(slot):
        if slot not in sent_six:
            sent_six[slot] = partial(1, slot, upper_six, lower_six, tilted, "rest")

    from_rest(0)
    beside_six = [[hop(sent_six[0][0], *aside)]] if skips else []
    for step in steps_to(far)[1:]:
        from_rest(slot_of(step, far))
    moving_six[far] = go_on(1, sent_six, moving_six[far], far)
    for slot in slots:
        from_rest(slot)
    sums_six = sums(1, upper_six, lower_six, local_six, occupation_six)
    for g in goals[1:]:
        moving_six[g] = go_on(1, sent_six, moving_six[g], g, [], last_cuts)
    updated_five = call(
        turn_kernel, [whole], [], [eigenbasis, turned, eigen_five], (), "back_five"
    )[0]
    own_six = call(
        finish_kernel,
        [whole],
        [occupation_six, bath_coefficients],
        [tilted, *sums_six, raised_six, lowered_six],
        (),
        "finish_six",
    )[0]
    previous = []
    for number in range(len(last_cuts)):
        last = [*[moving_six[g] for g in goals[1:]], moving_six[far], *beside_six]
        previous = solve_six(own_six, last, number, previous)
    return (updated_five, previous[0])


def solution(mesh):
    by_block = P(("ma", "mb"))
    in_specs = (by_block,) * 3 + (P(),) * 5 + (by_block,) * 8
    return jax.shard_map(
        body, mesh=mesh, in_specs=in_specs, out_specs=(by_block, by_block), check_vma=False
    )
```
